256 devices in a mesh: seq: 32 (over x, y, core), head: 8 (over z).
Axes of the slice: x: 4, y: 4, z: 8, core: 2. Of those that a mesh axis runs over, the one named last changes fastest.
Arguments:
- query_vectors: bfloat16 [32768, 4096], P('seq', 'head'), may hold values from -6 to 6
- key_vectors: bfloat16 [32768, 4096], P('seq', 'head'), may hold values from -6 to 6
- value_vectors: bfloat16 [32768, 4096], P('seq', 'head'), may hold values from -120 to 120
- send_slots: int32 [1024, 48], P('seq'), may hold values from 0 to 1024, as said below
- receive_slots: int32 [1024, 48], P('seq'), may hold values from 0 to 1024, as said below
- resets: int32 [256], P('seq'), may hold values 0 or 1
Outputs:
- attended: bfloat16 [32768, 4096], P('seq', 'head')
The draws below stay inside these ranges and needn't reach their ends.
Inputs may be any that keep to these rules, and one draw needn't show every extreme that they name: `send_slots`: row s * 32 + d lists in its first slots distinct local rows of device s that go to device d and holds 1024 in the rest; every local row of every device is listed once; no row has more than 48 live slots, and every device sends 48 rows to some device and receives 48 rows from some device. `receive_slots`: row d * 32 + s holds, slot for slot with row s * 32 + d of send_slots, distinct context positions on device d, and 1024 where that slot is empty; every position of every device is named once.
All inputs are finite; a program needn't handle non-finite values. No bound on the sum of `resets` on one device may be relied on, other than what follows from the above.
Results may differ from the reference program's by a relative error of at most 0.0049.
Values may be sent and summed in bfloat16 or wider, within the bound.
A program may use at most 64 MiB of HBM per device.

```python
import math
import jax
import jax.numpy as jnp
from jax import lax

H = 32
HD = 128
CH = 128
TOK_DEV = 1024
TOKENS = 32768
CAP = 48
NCHUNK = 256
N_SEQ = 32


def route_tables(key):
    key = jax.random.fold_in(key, 5)
    split_keys = jax.random.split(key, 5)
    remaining = TOK_DEV - CAP
    base_load = remaining // (N_SEQ - 1)
    leftover = remaining - base_load * (N_SEQ - 1)
    jitter_top = min(base_load, CAP - base_load - 1)
    slot_index = jnp.arange(N_SEQ - 1, dtype=jnp.int32)
    extra_one = (slot_index < leftover).astype(jnp.int32)
    jitter = jax.random.randint(split_keys[0], (N_SEQ // 2 + 1,), 0, jitter_top + 1)
    shift_terms = jitter[slot_index // 2] * jnp.where(slot_index % 2 == 0, 1, -1)
    if (N_SEQ - 1) % 2 == 1:
        shift_terms = jnp.where(slot_index == N_SEQ - 2, 0, shift_terms)
    pair_loads = jnp.concatenate([jnp.full((1,), CAP, jnp.int32), base_load + extra_one + shift_terms]).astype(jnp.int32)
    dest_perm = jax.random.permutation(split_keys[1], N_SEQ)
    source_perm = jax.random.permutation(split_keys[2], N_SEQ)
    counts = pair_loads[(dest_perm[None, :] - source_perm[:, None]) % N_SEQ]
    send_start = jnp.cumsum(counts, axis=1) - counts
    receive_start = jnp.cumsum(counts, axis=0) - counts
    send_perm = jax.vmap(lambda row_key: jax.random.permutation(row_key, TOK_DEV))(jax.random.split(split_keys[3], N_SEQ))
    receive_perm = jax.vmap(lambda row_key: jax.random.permutation(row_key, TOK_DEV))(jax.random.split(split_keys[4], N_SEQ))
    slot_range = jnp.arange(CAP, dtype=jnp.int32)
    live_slot = slot_range[None, None, :] < counts[:, :, None]
    device_range = jnp.arange(N_SEQ, dtype=jnp.int32)
    send_pick = jnp.clip(send_start[:, :, None] + slot_range[None, None, :], 0, TOK_DEV - 1)
    receive_pick = jnp.clip(receive_start[:, :, None] + slot_range[None, None, :], 0, TOK_DEV - 1)
    send_values = send_perm[device_range[:, None, None], send_pick]
    receive_values = receive_perm[device_range[None, :, None], receive_pick]
    send_table = jnp.where(live_slot, send_values, TOK_DEV).astype(jnp.int32).reshape(N_SEQ * N_SEQ, CAP)
    receive_table = jnp.transpose(jnp.where(live_slot, receive_values, TOK_DEV).astype(jnp.int32), (1, 0, 2)).reshape(N_SEQ * N_SEQ, CAP)
    return (send_table, receive_table)


def draw_send_slots(key, part):
    return route_tables(key)[0]


def draw_receive_slots(key, part):
    return route_tables(key)[1]


def draw_value_vectors(key, part):
    key = jax.random.fold_in(key, 11)
    noise_key, scale_key = jax.random.split(key)
    columns = jnp.arange(H * HD) // HD
    head_scale = 10.0 ** (columns.astype(jnp.float32) / max(H - 1, 1))
    noise = jnp.clip(jax.random.normal(noise_key, (TOKENS, H * HD), jnp.float32), -6.0, 6.0)
    row_scale = jnp.exp(jax.random.uniform(scale_key, (TOKENS, 1), jnp.float32, math.log(0.5), math.log(2.0)))
    return (noise * head_scale[None, :] * row_scale).astype(jnp.bfloat16)


def with_ends(values, own_key, smallest, high):
    extent = values.shape
    index_at = [jax.random.randint(jax.random.fold_in(own_key, axis), (), 0, extent[axis]) for axis in range(len(extent))]
    values = values.at[tuple(index_at)].set(smallest)
    longest = extent.index(max(extent))
    index_at[longest] = (index_at[longest] + 1) % extent[longest]
    return values.at[tuple(index_at)].set(high)


def shard_levels(stream_key, shape, cuts, least, largest):
    factor_of, own = 1.0, jax.random.fold_in(stream_key, 6)
    for position, shards_of in cuts:
        heights = jnp.exp(jax.random.uniform(jax.random.fold_in(own, position), (shards_of,), jnp.float32, least / len(cuts), largest / len(cuts)))
        factor_of = factor_of * jnp.repeat(heights, shape[position] // shards_of).reshape([-1 if axis == position else 1 for axis in range(len(shape))])
    return factor_of


def normal_values(key, shape, width, bound, cuts=(), held_as=jnp.bfloat16):
    drawn = jax.random.normal(key, shape, jnp.float32) * width
    if len(cuts) > 0:
        drawn = shard_levels(key, shape, cuts, -0.22, 0.18) * drawn
    return jnp.clip(drawn, min=-bound, max=bound).astype(held_as)


def setup_inputs(seed: int = 0) -> dict:
    key_list = jax.random.split(jax.random.key(seed), 7)
    return {
        "query_vectors": normal_values(key_list[0], (TOKENS, H * HD), 1.0, 6.0, ((0, 32), (1, 8))),
        "key_vectors": normal_values(key_list[1], (TOKENS, H * HD), 1.0, 6.0, ((0, 32), (1, 8))),
        "value_vectors": draw_value_vectors(jax.random.fold_in(key_list[6], 71), 0),
        "send_slots": draw_send_slots(jax.random.fold_in(key_list[6], 71), 0),
        "receive_slots": draw_receive_slots(jax.random.fold_in(key_list[6], 71), 0),
        "resets": with_ends((jax.random.randint(key_list[5], (NCHUNK,), 0, 4 * TOK_DEV // CH) < 1).astype(jnp.int32), jax.random.fold_in(key_list[5], 1), 0, 1),
    }


epsilon = 1e-05

def relocate(source_rows, from_index, to_index):
    row_width = source_rows.shape[1]
    padded = jnp.concatenate([source_rows, jnp.zeros((1, row_width), source_rows.dtype)], 0)
    moved = jnp.zeros((TOKENS + 1, row_width), source_rows.dtype).at[to_index].set(padded[from_index])
    return moved[:TOKENS]

def reference(query_vectors, key_vectors, value_vectors, send_slots, receive_slots, resets):
    row_width = H * HD
    send_table = send_slots.reshape(N_SEQ, N_SEQ, CAP)
    receive_table = jnp.transpose(receive_slots.reshape(N_SEQ, N_SEQ, CAP), (1, 0, 2))
    live_slot = send_table < TOK_DEV
    owner_index = jnp.arange(N_SEQ, dtype=jnp.int32)
    arrival_index = jnp.where(live_slot, owner_index[:, None, None] * TOK_DEV + send_table, TOKENS).reshape(-1).astype(jnp.int32)
    context_index = jnp.where(live_slot, owner_index[None, :, None] * TOK_DEV + receive_table, TOKENS).reshape(-1).astype(jnp.int32)
    q_ctx = relocate(query_vectors, arrival_index, context_index)
    k_ctx = relocate(key_vectors, arrival_index, context_index)
    v_ctx = relocate(value_vectors, arrival_index, context_index)
    causal = jnp.arange(CH)[:, None] >= jnp.arange(CH)[None, :]

    def group_step(carried, group_item):
        q_group, k_group, v_group, reset_flag = group_item
        q_heads = q_group.reshape(CH, H, HD).astype(jnp.float32)
        k_heads = k_group.reshape(CH, H, HD).astype(jnp.float32)
        v_heads = v_group.reshape(CH, H, HD).astype(jnp.float32)
        carried = jnp.where(reset_flag > 0, jnp.zeros_like(carried), carried)
        rounded = lax.optimization_barrier(carried.astype(jnp.bfloat16)).astype(jnp.float32)
        inter_term = jnp.einsum('thd,hde->the', q_heads, rounded)
        scores = jnp.einsum('thd,shd->hts', q_heads, k_heads)
        weights = lax.optimization_barrier(jnp.where(causal[None], scores, 0.0).astype(jnp.bfloat16)).astype(jnp.float32)
        intra_term = jnp.einsum('hts,she->the', weights, v_heads)
        raw_out = inter_term + intra_term
        mean_sq = lax.optimization_barrier(jnp.mean(raw_out * raw_out, axis=(1, 2)))
        normed = (raw_out * lax.rsqrt(mean_sq + epsilon)[:, None, None]).astype(jnp.bfloat16).reshape(CH, row_width)
        carried_next = carried + jnp.einsum('thd,the->hde', k_heads, v_heads)
        return (carried_next, normed)
    initial = jnp.zeros((H, HD, HD), jnp.float32)
    group_items = (q_ctx.reshape(NCHUNK, CH, row_width), k_ctx.reshape(NCHUNK, CH, row_width), v_ctx.reshape(NCHUNK, CH, row_width), resets)
    _, normed_all = lax.scan(group_step, initial, group_items)
    return relocate(normed_all.reshape(TOKENS, row_width), context_index, arrival_index)
```

```python
import functools

import jax
import jax.numpy as jnp
from jax import lax
from jax.experimental import pallas as pl
from jax.experimental.pallas import tpu as pltpu
from jax.sharding import PartitionSpec as P

H = 32
HD = 128
CH = 128
CAP = 48
N_SEQ = 32
N_HEAD = 8
TOK = 1024
WIDE = 512
COLS = 256
SLOTS = N_SEQ * CAP
GROUPS = TOK // CH
PIECE = COLS // N_SEQ
MESH = pl.DeviceIdType.MESH
BF16 = jnp.bfloat16
F32 = jnp.float32

epsilon = 1e-05

K0, V0, K1, V1, Q0, Q1, R0, R1 = range(8)


def kernel(
    q_ref, k_ref, v_ref, tab_ref, resets_ref, out_ref,
    pack_send, place_send, pack_recv, place_recv,
    outbox, inbox, q_ctx, k_ctx, v_ctx, raw, kv, carried, state_out, state_in, prefix_out, prefix_in,
    back, z_box,
    bulk_ssem, bulk_rsem, st_ssem, st_rsem, pf_ssem, pf_rsem, z_ssem, z_rsem,
):
    me = lax.axis_index("seq")
    mine = lax.axis_index("head")

    barrier = pltpu.get_barrier_semaphore()

    @pl.loop(1, N_SEQ)
    def _(k):
        pl.semaphore_signal(
            barrier, inc=1, device_id={"seq": lax.rem(me + k, N_SEQ), "head": mine}, device_id_type=MESH
        )

    @pl.loop(1, N_HEAD)
    def _(k):
        pl.semaphore_signal(
            barrier, inc=1, device_id={"seq": me, "head": lax.rem(mine + k, N_HEAD)}, device_id_type=MESH
        )

    diagonal = (
        lax.broadcasted_iota(jnp.int32, (128, 128), 0) == lax.broadcasted_iota(jnp.int32, (128, 128), 1)
    )

    def to_column(row):
        return jnp.sum(jnp.where(diagonal, jnp.broadcast_to(row, (128, 128)), 0.0), axis=1, keepdims=True)

    def to_row(column):
        return jnp.sum(jnp.where(diagonal, jnp.broadcast_to(column, (128, 128)), 0.0), axis=0, keepdims=True)

    def build_pack(table, pack):
        @pl.loop(0, SLOTS // 128)
        def _(i):
            column = to_column(tab_ref[pl.ds(table * 12 + i, 1), :].astype(F32))
            spots = lax.broadcasted_iota(jnp.int32, (128, TOK), 1).astype(F32)
            pack[pl.ds(pl.multiple_of(i * 128, 128), 128), :] = jnp.where(spots == column, 1.0, 0.0).astype(BF16)

    def build_place(table, place):
        for i in range(SLOTS // 128):
            row = tab_ref[table * 12 + i : table * 12 + i + 1, :]

            @pl.loop(0, TOK // 256)
            def _(j):
                spots = lax.broadcasted_iota(jnp.int32, (256, 128), 0) + j * 256
                place[pl.ds(pl.multiple_of(j * 256, 256), 256), i * 128 : (i + 1) * 128] = jnp.where(
                    spots == row, 1.0, 0.0
                ).astype(BF16)

    def pack_rows(pack, rows_ref, half, stage):
        @pl.loop(0, SLOTS // 384)
        def _(i):
            here = pl.ds(pl.multiple_of(i * 384, 384), 384)
            outbox[stage, here, :] = jnp.dot(
                pack[here, :], rows_ref[:, half * COLS : (half + 1) * COLS], preferred_element_type=F32
            ).astype(BF16)

    def place_rows(place, stage, rows_ref, half):
        @pl.loop(0, TOK // 256)
        def _(i):
            here = pl.ds(pl.multiple_of(i * 256, 256), 256)
            rows_ref[here, half * COLS : (half + 1) * COLS] = jnp.dot(
                place[here, :], inbox[stage], preferred_element_type=F32
            ).astype(BF16)

    def block(device):
        return pl.ds(pl.multiple_of(device * CAP, CAP), CAP)

    def send_bulk(stage):
        @pl.loop(1, N_SEQ)
        def _(k):
            peer = lax.rem(me + k, N_SEQ)
            pltpu.make_async_remote_copy(
                src_ref=outbox.at[stage, block(peer), :],
                dst_ref=inbox.at[stage, block(me), :],
                send_sem=bulk_ssem.at[stage],
                recv_sem=bulk_rsem.at[stage],
                device_id={"seq": peer, "head": mine},
                device_id_type=MESH,
            ).start()

        inbox[stage, block(me), :] = outbox[stage, block(me), :]

    def all_bulk(stage):
        most = pl.ds(0, SLOTS - CAP)
        return pltpu.make_async_remote_copy(
            src_ref=outbox.at[stage, most, :],
            dst_ref=inbox.at[stage, most, :],
            send_sem=bulk_ssem.at[stage],
            recv_sem=bulk_rsem.at[stage],
            device_id={"seq": me, "head": mine},
            device_id_type=MESH,
        )

    def send_small(source, target, half, ssem, rsem):
        @pl.loop(1, N_SEQ)
        def _(k):
            peer = lax.rem(me + k, N_SEQ)
            pltpu.make_async_remote_copy(
                src_ref=source.at[half, peer],
                dst_ref=target.at[half, me],
                send_sem=ssem.at[half],
                recv_sem=rsem.at[half],
                device_id={"seq": peer, "head": mine},
                device_id_type=MESH,
            ).start()

        target[half, me] = source[half, me]

    def all_small(source, target, half, ssem, rsem):
        return pltpu.make_async_remote_copy(
            src_ref=source.at[half, pl.ds(0, N_SEQ - 1)],
            dst_ref=target.at[half, pl.ds(0, N_SEQ - 1)],
            send_sem=ssem.at[half],
            recv_sem=rsem.at[half],
            device_id={"seq": me, "head": mine},
            device_id_type=MESH,
        )

    def keep_of(group):
        return 1.0 - resets_ref[group].astype(F32)

    def group_states(half):
        state = [jnp.zeros((HD, HD), F32), jnp.zeros((HD, HD), F32)]
        kept = jnp.float32(1.0)
        for c in range(GROUPS):
            keep = keep_of(c)
            kept = kept * keep
            for h in range(2):
                cols = slice(half * COLS + h * HD, half * COLS + (h + 1) * HD)
                rows = slice(c * CH, (c + 1) * CH)
                group_kv = lax.dot_general(
                    k_ctx[rows, cols], v_ctx[rows, cols], (((0,), (0,)), ((), ())), preferred_element_type=F32
                )
                kv[half, c, h * HD : (h + 1) * HD, :] = group_kv
                state[h] = state[h] * keep + group_kv
        for h in range(2):
            state_out[half, h * 16 : (h + 1) * 16, 0:PIECE, :] = state[h].reshape(16, PIECE, HD)
        state_out[half, :, PIECE : PIECE + 8, :] = jnp.broadcast_to(kept, (N_SEQ, 8, HD))

    def prefixes(half):
        total = jnp.zeros((PIECE, HD), F32)
        for s in range(N_SEQ):
            prefix_out[half, s] = total
            total = state_in[half, s, 0:PIECE, :] + state_in[half, s, PIECE : PIECE + 8, :] * total

    def attend(half):
        causal = (
            lax.broadcasted_iota(jnp.int32, (CH, CH), 0) >= lax.broadcasted_iota(jnp.int32, (CH, CH), 1)
        )
        for h in range(2):
            state = prefix_in[half, h * 16 : (h + 1) * 16].reshape(HD, HD)
            for c in range(GROUPS):
                state = state * keep_of(c)
                carried[half, c, h * HD : (h + 1) * HD, :] = state.astype(BF16)
                state = state + kv[half, c, h * HD : (h + 1) * HD, :]
        for c in range(GROUPS):
            for h in range(2):
                cols = slice(half * COLS + h * HD, half * COLS + (h + 1) * HD)
                rows = slice(c * CH, (c + 1) * CH)
                q = q_ctx[rows, cols]
                scores = lax.dot_general(
                    q, k_ctx[rows, cols], (((1,), (1,)), ((), ())), preferred_element_type=F32
                )
                weights = jnp.where(causal, scores, 0.0).astype(BF16)
                raw[rows, cols] = (
                    jnp.dot(q, carried[half, c, h * HD : (h + 1) * HD, :], preferred_element_type=F32)
                    + jnp.dot(weights, v_ctx[rows, cols], preferred_element_type=F32)
                ).astype(BF16)

    build_pack(0, pack_send)
    pack_rows(pack_send, k_ref, 0, K0)
    pl.semaphore_wait(barrier, N_SEQ - 1 + N_HEAD - 1)
    send_bulk(K0)
    pack_rows(pack_send, v_ref, 0, V0)
    send_bulk(V0)
    pack_rows(pack_send, k_ref, 1, K1)
    build_place(1, place_recv)
    pack_rows(pack_send, v_ref, 1, V1)
    all_bulk(K0).wait_send()
    send_bulk(K1)
    pack_rows(pack_send, q_ref, 0, Q0)
    pack_rows(pack_send, q_ref, 1, Q1)
    build_pack(1, pack_recv)
    build_place(0, place_send)
    all_bulk(K0).wait_recv()
    place_rows(place_recv, K0, k_ctx, 0)
    all_bulk(V0).wait_send()
    send_bulk(V1)
    all_bulk(V0).wait_recv()
    place_rows(place_recv, V0, v_ctx, 0)
    group_states(0)
    send_small(state_out, state_in, 0, st_ssem, st_rsem)
    all_bulk(K1).wait_send()
    send_bulk(Q0)
    all_small(state_out, state_in, 0, st_ssem, st_rsem).wait_recv()
    prefixes(0)
    send_small(prefix_out, prefix_in, 0, pf_ssem, pf_rsem)
    all_bulk(K1).wait_recv()
    place_rows(place_recv, K1, k_ctx, 1)
    all_bulk(V1).wait_send()
    send_bulk(Q1)
    all_bulk(V1).wait_recv()
    place_rows(place_recv, V1, v_ctx, 1)
    group_states(1)
    send_small(state_out, state_in, 1, st_ssem, st_rsem)
    all_small(state_out, state_in, 1, st_ssem, st_rsem).wait_recv()
    prefixes(1)
    send_small(prefix_out, prefix_in, 1, pf_ssem, pf_rsem)
    all_small(prefix_out, prefix_in, 0, pf_ssem, pf_rsem).wait_recv()
    all_bulk(Q0).wait_recv()
    place_rows(place_recv, Q0, q_ctx, 0)
    attend(0)
    pack_rows(pack_recv, raw, 0, R0)
    send_bulk(R0)
    all_small(prefix_out, prefix_in, 1, pf_ssem, pf_rsem).wait_recv()
    all_bulk(Q1).wait_recv()
    place_rows(place_recv, Q1, q_ctx, 1)
    attend(1)
    pack_rows(pack_recv, raw, 1, R1)
    send_bulk(R1)
    all_bulk(R0).wait_recv()
    place_rows(place_send, R0, back, 0)
    all_bulk(R1).wait_recv()
    place_rows(place_send, R1, back, 1)

    for c in range(TOK // 128):
        rows = back[c * 128 : (c + 1) * 128, :].astype(F32)
        z_box[mine, c : c + 1, :] = to_row(jnp.sum(rows * rows, axis=1, keepdims=True))

    @pl.loop(1, N_HEAD)
    def _(k):
        pltpu.make_async_remote_copy(
            src_ref=z_box.at[mine],
            dst_ref=z_box.at[mine],
            send_sem=z_ssem,
            recv_sem=z_rsem,
            device_id={"seq": me, "head": lax.rem(mine + k, N_HEAD)},
            device_id_type=MESH,
        ).start()

    all_z = pltpu.make_async_remote_copy(
        src_ref=z_box.at[pl.ds(0, N_HEAD - 1)],
        dst_ref=z_box.at[pl.ds(0, N_HEAD - 1)],
        send_sem=z_ssem,
        recv_sem=z_rsem,
        device_id={"seq": me, "head": mine},
        device_id_type=MESH,
    )
    all_z.wait_recv()
    squares = z_box[0]
    for z in range(1, N_HEAD):
        squares = squares + z_box[z]
    scale = lax.rsqrt(squares / (H * HD) + epsilon)
    for c in range(TOK // 128):
        rows = slice(c * 128, (c + 1) * 128)
        out_ref[rows, :] = (back[rows, :].astype(F32) * to_column(scale[c : c + 1, :])).astype(BF16)

    all_z.wait_send()
    for stage in (Q0, Q1, R0, R1):
        all_bulk(stage).wait_send()
    for half in range(2):
        all_small(state_out, state_in, half, st_ssem, st_rsem).wait_send()
        all_small(prefix_out, prefix_in, half, pf_ssem, pf_rsem).wait_send()


def shards(query_vectors, key_vectors, value_vectors, send_slots, receive_slots, resets):
    tables = jnp.concatenate([send_slots.reshape(SLOTS // 128, 128), receive_slots.reshape(SLOTS // 128, 128)], 0)
    vmem = pl.BlockSpec(memory_space=pltpu.VMEM)
    square = lambda rows, columns: pltpu.VMEM((rows, columns), BF16)
    return pl.pallas_call(
        kernel,
        name="attention",
        out_shape=jax.ShapeDtypeStruct((TOK, WIDE), BF16),
        in_specs=[vmem, vmem, vmem, vmem, pl.BlockSpec(memory_space=pltpu.SMEM)],
        out_specs=vmem,
        scratch_shapes=[
            square(SLOTS, TOK), square(TOK, SLOTS), square(SLOTS, TOK), square(TOK, SLOTS),
            pltpu.VMEM((8, SLOTS, COLS), BF16), pltpu.VMEM((8, SLOTS, COLS), BF16),
            square(TOK, WIDE), square(TOK, WIDE), square(TOK, WIDE), square(TOK, WIDE),
            pltpu.VMEM((2, GROUPS, COLS, HD), F32), pltpu.VMEM((2, GROUPS, COLS, HD), BF16),
            pltpu.VMEM((2, N_SEQ, PIECE + 8, HD), F32), pltpu.VMEM((2, N_SEQ, PIECE + 8, HD), F32),
            pltpu.VMEM((2, N_SEQ, PIECE, HD), F32), pltpu.VMEM((2, N_SEQ, PIECE, HD), F32),
            square(TOK, WIDE), pltpu.VMEM((N_HEAD, TOK // 128, 128), F32),
            pltpu.SemaphoreType.DMA((8,)), pltpu.SemaphoreType.DMA((8,)),
            pltpu.SemaphoreType.DMA((2,)), pltpu.SemaphoreType.DMA((2,)),
            pltpu.SemaphoreType.DMA((2,)), pltpu.SemaphoreType.DMA((2,)),
            pltpu.SemaphoreType.DMA, pltpu.SemaphoreType.DMA,
        ],
        compiler_params=pltpu.CompilerParams(
            collective_id=0, has_side_effects=True, vmem_limit_bytes=56 * 2**20
        ),
    )(query_vectors, key_vectors, value_vectors, tables, resets)


def solution(mesh):
    placed = (
        P("seq", "head"),
        P("seq", "head"),
        P("seq", "head"),
        P("seq", None),
        P("seq", None),
        P("seq"),
    )
    return jax.shard_map(shards, mesh=mesh, in_specs=placed, out_specs=P("seq", "head"), check_vma=False)
```

```python
import functools

import jax
import jax.numpy as jnp
from jax import lax
from jax.experimental import pallas as pl
from jax.experimental.pallas import tpu as pltpu
from jax.sharding import PartitionSpec as P

H = 32
HD = 128
CH = 128
CAP = 48
N_SEQ = 32
N_HEAD = 8
TOK = 1024
WIDE = 512
COLS = 256
SLOTS = N_SEQ * CAP
GROUPS = TOK // CH
PIECE = COLS // N_SEQ
MESH = pl.DeviceIdType.MESH
BF16 = jnp.bfloat16
F32 = jnp.float32

epsilon = 1e-05

K0, V0, K1, V1, Q0, Q1, R0, R1 = range(8)


def kernel(
    q_hbm, k_hbm, v_hbm, send_ref, receive_ref, resets_ref, back, scale_ref,
    q_ref, k_ref, v_ref, columns,
    pack_send, place_send, pack_recv, place_recv,
    outbox, inbox, q_ctx, k_ctx, v_ctx, raw, kv, carried, state_out, state_in, prefix_out, prefix_in,
    z_box, in_sem,
    bulk_ssem, bulk_rsem, st_ssem, st_rsem, pf_ssem, pf_rsem, z_ssem, z_rsem,
):
    me = lax.axis_index("seq")
    mine = lax.axis_index("head")

    barrier = pltpu.get_barrier_semaphore()

    @pl.loop(1, N_SEQ)
    def _(k):
        pl.semaphore_signal(
            barrier, inc=1, device_id={"seq": lax.rem(me + k, N_SEQ), "head": mine}, device_id_type=MESH
        )

    @pl.loop(1, N_HEAD)
    def _(k):
        pl.semaphore_signal(
            barrier, inc=1, device_id={"seq": me, "head": lax.rem(mine + k, N_HEAD)}, device_id_type=MESH
        )

    staged = [
        pltpu.make_async_copy(source, target, in_sem.at[i])
        for i, (source, target) in enumerate([(k_hbm, k_ref), (v_hbm, v_ref), (q_hbm, q_ref)])
    ]
    for copy in staged:
        copy.start()

    diagonal = (
        lax.broadcasted_iota(jnp.int32, (128, 128), 0) == lax.broadcasted_iota(jnp.int32, (128, 128), 1)
    )

    def to_column(row):
        return jnp.sum(jnp.where(diagonal, jnp.broadcast_to(row, (128, 128)), 0.0), axis=1, keepdims=True)

    def to_row(column):
        return jnp.sum(jnp.where(diagonal, jnp.broadcast_to(column, (128, 128)), 0.0), axis=0, keepdims=True)

    def build_pack(table_ref, pack):
        corner = diagonal[:CAP, :CAP]
        for d in range(N_SEQ):
            row = jnp.broadcast_to(table_ref[d : d + 1, :].astype(F32), (CAP, CAP))
            column = jnp.sum(jnp.where(corner, row, 0.0), axis=1, keepdims=True)
            spots = lax.broadcasted_iota(jnp.int32, (CAP, TOK), 1).astype(F32)
            pack[d * CAP : (d + 1) * CAP, :] = jnp.where(spots == column, 1.0, 0.0).astype(BF16)
            columns[d * CAP : (d + 1) * CAP, :] = column

    def build_place(place):
        for i in range(SLOTS // 128):
            row = to_row(columns[i * 128 : (i + 1) * 128, :])

            @pl.loop(0, TOK // 256)
            def _(j):
                spots = (lax.broadcasted_iota(jnp.int32, (256, 128), 0) + j * 256).astype(F32)
                place[pl.ds(pl.multiple_of(j * 256, 256), 256), i * 128 : (i + 1) * 128] = jnp.where(
                    spots == row, 1.0, 0.0
                ).astype(BF16)

    def pack_rows(pack, rows_ref, half, stage):
        @pl.loop(0, SLOTS // 384)
        def _(i):
            here = pl.ds(pl.multiple_of(i * 384, 384), 384)
            outbox[stage, here, :] = jnp.dot(
                pack[here, :], rows_ref[:, half * COLS : (half + 1) * COLS], preferred_element_type=F32
            ).astype(BF16)

    def place_rows(place, stage, rows_ref, half):
        @pl.loop(0, TOK // 256)
        def _(i):
            here = pl.ds(pl.multiple_of(i * 256, 256), 256)
            rows_ref[here, half * COLS : (half + 1) * COLS] = jnp.dot(
                place[here, :], inbox[stage], preferred_element_type=F32
            ).astype(BF16)

    def block(device):
        return pl.ds(pl.multiple_of(device * CAP, CAP), CAP)

    def send_bulk(stage):
        @pl.loop(1, N_SEQ)
        def _(k):
            peer = lax.rem(me + 13 * k, N_SEQ)
            pltpu.make_async_remote_copy(
                src_ref=outbox.at[stage, block(peer), :],
                dst_ref=inbox.at[stage, block(me), :],
                send_sem=bulk_ssem.at[stage],
                recv_sem=bulk_rsem.at[stage],
                device_id={"seq": peer, "head": mine},
                device_id_type=MESH,
            ).start()

        inbox[stage, block(me), :] = outbox[stage, block(me), :]

    def all_bulk(stage):
        most = pl.ds(0, SLOTS - CAP)
        return pltpu.make_async_remote_copy(
            src_ref=outbox.at[stage, most, :],
            dst_ref=inbox.at[stage, most, :],
            send_sem=bulk_ssem.at[stage],
            recv_sem=bulk_rsem.at[stage],
            device_id={"seq": me, "head": mine},
            device_id_type=MESH,
        )

    def send_small(source, target, half, ssem, rsem):
        @pl.loop(1, N_SEQ)
        def _(k):
            peer = lax.rem(me + 13 * k, N_SEQ)
            pltpu.make_async_remote_copy(
                src_ref=source.at[half, peer],
                dst_ref=target.at[half, me],
                send_sem=ssem.at[half],
                recv_sem=rsem.at[half],
                device_id={"seq": peer, "head": mine},
                device_id_type=MESH,
            ).start()

        target[half, me] = source[half, me]

    def all_small(source, target, half, ssem, rsem):
        return pltpu.make_async_remote_copy(
            src_ref=source.at[half, pl.ds(0, N_SEQ - 1)],
            dst_ref=target.at[half, pl.ds(0, N_SEQ - 1)],
            send_sem=ssem.at[half],
            recv_sem=rsem.at[half],
            device_id={"seq": me, "head": mine},
            device_id_type=MESH,
        )

    def keep_of(group):
        return 1.0 - resets_ref[group].astype(F32)

    def group_states(half):
        state = [jnp.zeros((HD, HD), F32), jnp.zeros((HD, HD), F32)]
        kept = jnp.float32(1.0)
        for c in range(GROUPS):
            keep = keep_of(c)
            kept = kept * keep
            for h in range(2):
                cols = slice(half * COLS + h * HD, half * COLS + (h + 1) * HD)
                rows = slice(c * CH, (c + 1) * CH)
                group_kv = lax.dot_general(
                    k_ctx[rows, cols], v_ctx[rows, cols], (((0,), (0,)), ((), ())), preferred_element_type=F32
                )
                kv[half, c, h * HD : (h + 1) * HD, :] = group_kv
                state[h] = state[h] * keep + group_kv
        for h in range(2):
            state_out[half, h * 16 : (h + 1) * 16, 0:PIECE, :] = state[h].reshape(16, PIECE, HD)
        state_out[half, :, PIECE : PIECE + 8, :] = jnp.broadcast_to(kept, (N_SEQ, 8, HD))

    def prefixes(half):
        total = jnp.zeros((PIECE, HD), F32)
        for s in range(N_SEQ):
            prefix_out[half, s] = total
            total = state_in[half, s, 0:PIECE, :] + state_in[half, s, PIECE : PIECE + 8, :] * total

    def attend(half):
        causal = (
            lax.broadcasted_iota(jnp.int32, (CH, CH), 0) >= lax.broadcasted_iota(jnp.int32, (CH, CH), 1)
        )
        for h in range(2):
            state = prefix_in[half, h * 16 : (h + 1) * 16].reshape(HD, HD)
            for c in range(GROUPS):
                state = state * keep_of(c)
                carried[half, c, h * HD : (h + 1) * HD, :] = state.astype(BF16)
                state = state + kv[half, c, h * HD : (h + 1) * HD, :]
        for c in range(GROUPS):
            for h in range(2):
                cols = slice(half * COLS + h * HD, half * COLS + (h + 1) * HD)
                rows = slice(c * CH, (c + 1) * CH)
                q = q_ctx[rows, cols]
                scores = lax.dot_general(
                    q, k_ctx[rows, cols], (((1,), (1,)), ((), ())), preferred_element_type=F32
                )
                weights = jnp.where(causal, scores, 0.0).astype(BF16)
                raw[rows, cols] = (
                    jnp.dot(q, carried[half, c, h * HD : (h + 1) * HD, :], preferred_element_type=F32)
                    + jnp.dot(weights, v_ctx[rows, cols], preferred_element_type=F32)
                ).astype(BF16)

    build_pack(send_ref, pack_send)
    staged[0].wait()
    pack_rows(pack_send, k_ref, 0, K0)
    staged[1].wait()
    pack_rows(pack_send, v_ref, 0, V0)
    pl.semaphore_wait(barrier, N_SEQ - 1 + N_HEAD - 1)
    send_bulk(K0)
    send_bulk(V0)
    build_place(place_send)
    pack_rows(pack_send, k_ref, 1, K1)
    pack_rows(pack_send, v_ref, 1, V1)
    all_bulk(K0).wait_send()
    send_bulk(K1)
    staged[2].wait()
    pack_rows(pack_send, q_ref, 0, Q0)
    pack_rows(pack_send, q_ref, 1, Q1)
    build_pack(receive_ref, pack_recv)
    build_place(place_recv)
    all_bulk(K0).wait_recv()
    place_rows(place_recv, K0, k_ctx, 0)
    all_bulk(V0).wait_send()
    send_bulk(V1)
    all_bulk(V0).wait_recv()
    place_rows(place_recv, V0, v_ctx, 0)
    group_states(0)
    send_small(state_out, state_in, 0, st_ssem, st_rsem)
    all_bulk(K1).wait_send()
    send_bulk(Q0)
    all_small(state_out, state_in, 0, st_ssem, st_rsem).wait_recv()
    prefixes(0)
    send_small(prefix_out, prefix_in, 0, pf_ssem, pf_rsem)
    all_bulk(K1).wait_recv()
    place_rows(place_recv, K1, k_ctx, 1)
    all_bulk(V1).wait_send()
    send_bulk(Q1)
    all_bulk(V1).wait_recv()
    place_rows(place_recv, V1, v_ctx, 1)
    group_states(1)
    send_small(state_out, state_in, 1, st_ssem, st_rsem)
    all_small(state_out, state_in, 1, st_ssem, st_rsem).wait_recv()
    prefixes(1)
    send_small(prefix_out, prefix_in, 1, pf_ssem, pf_rsem)
    all_small(prefix_out, prefix_in, 0, pf_ssem, pf_rsem).wait_recv()
    all_bulk(Q0).wait_recv()
    place_rows(place_recv, Q0, q_ctx, 0)
    attend(0)
    pack_rows(pack_recv, raw, 0, R0)
    send_bulk(R0)
    all_small(prefix_out, prefix_in, 1, pf_ssem, pf_rsem).wait_recv()
    all_bulk(Q1).wait_recv()
    place_rows(place_recv, Q1, q_ctx, 1)
    attend(1)
    pack_rows(pack_recv, raw, 1, R1)
    send_bulk(R1)
    all_bulk(R0).wait_recv()
    place_rows(place_send, R0, back, 0)
    all_bulk(R1).wait_recv()
    place_rows(place_send, R1, back, 1)

    for c in range(TOK // 128):
        rows = back[c * 128 : (c + 1) * 128, :].astype(F32)
        z_box[mine, c : c + 1, :] = to_row(jnp.sum(rows * rows, axis=1, keepdims=True))

    @pl.loop(1, N_HEAD)
    def _(k):
        pltpu.make_async_remote_copy(
            src_ref=z_box.at[mine],
            dst_ref=z_box.at[mine],
            send_sem=z_ssem,
            recv_sem=z_rsem,
            device_id={"seq": me, "head": lax.rem(mine + k, N_HEAD)},
            device_id_type=MESH,
        ).start()

    all_z = pltpu.make_async_remote_copy(
        src_ref=z_box.at[pl.ds(0, N_HEAD - 1)],
        dst_ref=z_box.at[pl.ds(0, N_HEAD - 1)],
        send_sem=z_ssem,
        recv_sem=z_rsem,
        device_id={"seq": me, "head": mine},
        device_id_type=MESH,
    )
    all_z.wait_recv()
    squares = z_box[0]
    for z in range(1, N_HEAD):
        squares = squares + z_box[z]
    scale_ref[...] = lax.rsqrt(squares / (H * HD) + epsilon)

    all_z.wait_send()
    for stage in (Q0, Q1, R0, R1):
        all_bulk(stage).wait_send()
    for half in range(2):
        all_small(state_out, state_in, half, st_ssem, st_rsem).wait_send()
        all_small(prefix_out, prefix_in, half, pf_ssem, pf_rsem).wait_send()


def scale_rows(back_ref, scale_ref, out_ref):
    diagonal = (
        lax.broadcasted_iota(jnp.int32, (128, 128), 0) == lax.broadcasted_iota(jnp.int32, (128, 128), 1)
    )
    for c in range(TOK // 128):
        rows = slice(c * 128, (c + 1) * 128)
        spread = jnp.broadcast_to(scale_ref[c : c + 1, :], (128, 128))
        column = jnp.sum(jnp.where(diagonal, spread, 0.0), axis=1, keepdims=True)
        out_ref[rows, :] = (back_ref[rows, :].astype(F32) * column).astype(BF16)


def shards(query_vectors, key_vectors, value_vectors, send_slots, receive_slots, resets):
    vmem = pl.BlockSpec(memory_space=pltpu.VMEM)
    hbm = pl.BlockSpec(memory_space=pl.ANY)
    square = lambda rows, columns: pltpu.VMEM((rows, columns), BF16)
    back, scale = pl.pallas_call(
        kernel,
        name="attention",
        out_shape=[
            jax.ShapeDtypeStruct((TOK, WIDE), BF16),
            jax.ShapeDtypeStruct((TOK // 128, 128), F32),
        ],
        in_specs=[hbm, hbm, hbm, vmem, vmem, pl.BlockSpec(memory_space=pltpu.SMEM)],
        out_specs=[vmem, vmem],
        scratch_shapes=[
            square(TOK, WIDE), square(TOK, WIDE), square(TOK, WIDE), pltpu.VMEM((SLOTS, 1), F32),
            square(SLOTS, TOK), square(TOK, SLOTS), square(SLOTS, TOK), square(TOK, SLOTS),
            pltpu.VMEM((8, SLOTS, COLS), BF16), pltpu.VMEM((8, SLOTS, COLS), BF16),
            square(TOK, WIDE), square(TOK, WIDE), square(TOK, WIDE), square(TOK, WIDE),
            pltpu.VMEM((2, GROUPS, COLS, HD), F32), pltpu.VMEM((2, GROUPS, COLS, HD), BF16),
            pltpu.VMEM((2, N_SEQ, PIECE + 8, HD), F32), pltpu.VMEM((2, N_SEQ, PIECE + 8, HD), F32),
            pltpu.VMEM((2, N_SEQ, PIECE, HD), F32), pltpu.VMEM((2, N_SEQ, PIECE, HD), F32),
            pltpu.VMEM((N_HEAD, TOK // 128, 128), F32), pltpu.SemaphoreType.DMA((3,)),
            pltpu.SemaphoreType.DMA((8,)), pltpu.SemaphoreType.DMA((8,)),
            pltpu.SemaphoreType.DMA((2,)), pltpu.SemaphoreType.DMA((2,)),
            pltpu.SemaphoreType.DMA((2,)), pltpu.SemaphoreType.DMA((2,)),
            pltpu.SemaphoreType.DMA, pltpu.SemaphoreType.DMA,
        ],
        compiler_params=pltpu.CompilerParams(
            collective_id=0, has_side_effects=True, vmem_limit_bytes=60 * 2**20
        ),
    )(query_vectors, key_vectors, value_vectors, send_slots, receive_slots, resets)
    return pl.pallas_call(
        scale_rows,
        name="scale",
        out_shape=jax.ShapeDtypeStruct((TOK, WIDE), BF16),
        in_specs=[vmem, vmem],
        out_specs=vmem,
    )(back, scale)


def solution(mesh):
    placed = (
        P("seq", "head"),
        P("seq", "head"),
        P("seq", "head"),
        P("seq", None),
        P("seq", None),
        P("seq"),
    )
    return jax.shard_map(shards, mesh=mesh, in_specs=placed, out_specs=P("seq", "head"), check_vma=False)
```

```python
import functools

import jax
import jax.numpy as jnp
from jax import lax
from jax.experimental import pallas as pl
from jax.experimental.pallas import tpu as pltpu
from jax.sharding import PartitionSpec as P

H = 32
HD = 128
CH = 128
CAP = 48
N_SEQ = 32
N_HEAD = 8
TOK = 1024
WIDE = 512
COLS = 256
SLOTS = N_SEQ * CAP
GROUPS = TOK // CH
PIECE = COLS // N_SEQ
EARLY = 16
MESH = pl.DeviceIdType.MESH
BF16 = jnp.bfloat16
F32 = jnp.float32

epsilon = 1e-05

K0, V0, K1, V1, Q0, Q1, R0, R1 = range(8)


def kernel(
    q_hbm, k_hbm, v_hbm, send_ref, receive_ref, resets_ref, out_ref,
    q_ref, k_ref, v_ref, columns,
    pack_send, place_send, pack_recv, place_recv,
    outbox, inbox, q_ctx, k_ctx, v_ctx, raw, late_raw, kv, carried,
    state_out, state_in, prefix_out, prefix_in, keeps, scale_out, scale_in, scale_parts, partial, z_box,
    in_sem, bulk_ssem, bulk_rsem, st_ssem, st_rsem, pf_ssem, pf_rsem, row_ssem, row_rsem, z_ssem, z_rsem,
):
    me = lax.axis_index("seq")
    mine = lax.axis_index("head")

    barrier = pltpu.get_barrier_semaphore()

    @pl.loop(1, N_SEQ)
    def _(k):
        pl.semaphore_signal(
            barrier, inc=1, device_id={"seq": lax.rem(me + k, N_SEQ), "head": mine}, device_id_type=MESH
        )

    @pl.loop(1, N_HEAD)
    def _(k):
        pl.semaphore_signal(
            barrier, inc=1, device_id={"seq": me, "head": lax.rem(mine + k, N_HEAD)}, device_id_type=MESH
        )

    staged = [
        pltpu.make_async_copy(source, target, in_sem.at[i])
        for i, (source, target) in enumerate([(k_hbm, k_ref), (v_hbm, v_ref), (q_hbm, q_ref)])
    ]
    for copy in staged:
        copy.start()

    diagonal = (
        lax.broadcasted_iota(jnp.int32, (128, 128), 0) == lax.broadcasted_iota(jnp.int32, (128, 128), 1)
    )

    def to_column(row):
        return jnp.sum(jnp.where(diagonal, jnp.broadcast_to(row, (128, 128)), 0.0), axis=1, keepdims=True)

    def to_row(column):
        return jnp.sum(jnp.where(diagonal, jnp.broadcast_to(column, (128, 128)), 0.0), axis=0, keepdims=True)

    def build_pack(table_ref, pack):
        corner = diagonal[:CAP, :CAP]
        for d in range(N_SEQ):
            row = jnp.broadcast_to(table_ref[d : d + 1, :].astype(F32), (CAP, CAP))
            column = jnp.sum(jnp.where(corner, row, 0.0), axis=1, keepdims=True)
            spots = lax.broadcasted_iota(jnp.int32, (CAP, TOK), 1).astype(F32)
            pack[d * CAP : (d + 1) * CAP, :] = jnp.where(spots == column, 1.0, 0.0).astype(BF16)
            columns[d * CAP : (d + 1) * CAP, :] = column

    def build_place(place):
        for i in range(SLOTS // 128):
            row = to_row(columns[i * 128 : (i + 1) * 128, :])

            @pl.loop(0, TOK // 256)
            def _(j):
                spots = (lax.broadcasted_iota(jnp.int32, (256, 128), 0) + j * 256).astype(F32)
                place[pl.ds(pl.multiple_of(j * 256, 256), 256), i * 128 : (i + 1) * 128] = jnp.where(
                    spots == row, 1.0, 0.0
                ).astype(BF16)

    def pack_rows(pack, rows_ref, half, stage):
        @pl.loop(0, SLOTS // 384)
        def _(i):
            here = pl.ds(pl.multiple_of(i * 384, 384), 384)
            outbox[stage, here, :] = jnp.dot(
                pack[here, :], rows_ref[:, half * COLS : (half + 1) * COLS], preferred_element_type=F32
            ).astype(BF16)

    def place_rows(place, stage, rows_ref, half):
        @pl.loop(0, TOK // 256)
        def _(i):
            here = pl.ds(pl.multiple_of(i * 256, 256), 256)
            rows_ref[here, half * COLS : (half + 1) * COLS] = jnp.dot(
                place[here, :], inbox[stage], preferred_element_type=F32
            ).astype(BF16)

    def block(device):
        return pl.ds(pl.multiple_of(device * CAP, CAP), CAP)

    def send_bulk(stage, parts=(0, 1)):
        def send(part):
            def one(k):
                peer = lax.rem(me + 13 * k, N_SEQ)
                pltpu.make_async_remote_copy(
                    src_ref=outbox.at[stage, block(peer), :],
                    dst_ref=inbox.at[stage, block(me), :],
                    send_sem=bulk_ssem.at[stage, part],
                    recv_sem=bulk_rsem.at[stage],
                    device_id={"seq": peer, "head": mine},
                    device_id_type=MESH,
                ).start()

            return one

        if 0 in parts:
            pl.loop(1, EARLY + 1)(send(0))
            inbox[stage, block(me), :] = outbox[stage, block(me), :]
        if 1 in parts:
            pl.loop(EARLY + 1, N_SEQ)(send(1))

    def bulk_of(stage, blocks, part):
        rows = pl.ds(0, blocks * CAP)
        return pltpu.make_async_remote_copy(
            src_ref=outbox.at[stage, rows, :],
            dst_ref=inbox.at[stage, rows, :],
            send_sem=bulk_ssem.at[stage, part],
            recv_sem=bulk_rsem.at[stage],
            device_id={"seq": me, "head": mine},
            device_id_type=MESH,
        )

    def arrived(stage):
        bulk_of(stage, N_SEQ - 1, 0).wait_recv()

    def sent_early(stage):
        bulk_of(stage, EARLY, 0).wait_send()

    def sent_late(stage):
        bulk_of(stage, N_SEQ - 1 - EARLY, 1).wait_send()

    def send_small(source, target, half, ssem, rsem):
        @pl.loop(1, N_SEQ)
        def _(k):
            peer = lax.rem(me + 13 * k, N_SEQ)
            pltpu.make_async_remote_copy(
                src_ref=source.at[half, peer],
                dst_ref=target.at[half, me],
                send_sem=ssem.at[half],
                recv_sem=rsem.at[half],
                device_id={"seq": peer, "head": mine},
                device_id_type=MESH,
            ).start()

        target[half, me] = source[half, me]

    def all_small(source, target, half, ssem, rsem):
        return pltpu.make_async_remote_copy(
            src_ref=source.at[half, pl.ds(0, N_SEQ - 1)],
            dst_ref=target.at[half, pl.ds(0, N_SEQ - 1)],
            send_sem=ssem.at[half],
            recv_sem=rsem.at[half],
            device_id={"seq": me, "head": mine},
            device_id_type=MESH,
        )

    def send_rows(source_of, target, which):
        @pl.loop(1, N_SEQ)
        def _(k):
            peer = lax.rem(me + 13 * k, N_SEQ)
            pltpu.make_async_remote_copy(
                src_ref=source_of(peer),
                dst_ref=target.at[me],
                send_sem=row_ssem.at[which],
                recv_sem=row_rsem.at[which],
                device_id={"seq": peer, "head": mine},
                device_id_type=MESH,
            ).start()

    def all_rows(target, which):
        most = pl.ds(0, N_SEQ - 1)
        return pltpu.make_async_remote_copy(
            src_ref=target.at[most],
            dst_ref=target.at[most],
            send_sem=row_ssem.at[which],
            recv_sem=row_rsem.at[which],
            device_id={"seq": me, "head": mine},
            device_id_type=MESH,
        )

    def keep_of(group):
        return 1.0 - resets_ref[group].astype(F32)

    def group_states(half):
        state = [jnp.zeros((HD, HD), F32), jnp.zeros((HD, HD), F32)]
        for c in range(GROUPS):
            keep = keep_of(c)
            for h in range(2):
                cols = slice(half * COLS + h * HD, half * COLS + (h + 1) * HD)
                rows = slice(c * CH, (c + 1) * CH)
                group_kv = lax.dot_general(
                    k_ctx[rows, cols], v_ctx[rows, cols], (((0,), (0,)), ((), ())), preferred_element_type=F32
                )
                kv[half, c, h * HD : (h + 1) * HD, :] = group_kv
                state[h] = state[h] * keep + group_kv
        for h in range(2):
            state_out[half, h * 16 : (h + 1) * 16] = state[h].reshape(16, PIECE, HD)

    def prefixes(half):
        total = jnp.zeros((PIECE, HD), F32)
        for s in range(N_SEQ):
            prefix_out[half, s] = total
            total = state_in[half, s] + keeps[s] * total

    def attend(half):
        causal = (
            lax.broadcasted_iota(jnp.int32, (CH, CH), 0) >= lax.broadcasted_iota(jnp.int32, (CH, CH), 1)
        )
        for h in range(2):
            state = prefix_in[half, h * 16 : (h + 1) * 16].reshape(HD, HD)
            for c in range(GROUPS):
                state = state * keep_of(c)
                carried[half, c, h * HD : (h + 1) * HD, :] = state.astype(BF16)
                state = state + kv[half, c, h * HD : (h + 1) * HD, :]
        for c in range(GROUPS):
            rows = slice(c * CH, (c + 1) * CH)
            squares = jnp.zeros((CH, HD), F32)
            for h in range(2):
                cols = slice(half * COLS + h * HD, half * COLS + (h + 1) * HD)
                q = q_ctx[rows, cols]
                scores = lax.dot_general(
                    q, k_ctx[rows, cols], (((1,), (1,)), ((), ())), preferred_element_type=F32
                )
                weights = jnp.where(causal, scores, 0.0).astype(BF16)
                value = jnp.dot(q, carried[half, c, h * HD : (h + 1) * HD, :], preferred_element_type=F32)
                value = value + jnp.dot(weights, v_ctx[rows, cols], preferred_element_type=F32)
                squares = squares + value * value
                if half == 0:
                    raw[rows, cols] = value.astype(BF16)
                else:
                    late_raw[rows, h * HD : (h + 1) * HD] = value
            row = to_row(jnp.sum(squares, axis=1, keepdims=True))
            if half == 0:
                partial[c : c + 1, :] = row
            else:
                z_box[mine, c : c + 1, :] = partial[c : c + 1, :] + row

    slots = (
        lax.broadcasted_iota(jnp.int32, (CAP, 128), 0) == lax.broadcasted_iota(jnp.int32, (CAP, 128), 1)
    )

    def normalize(scale):
        lane = lax.broadcasted_iota(jnp.int32, (128, 128), 1)
        for c in range(TOK // 128):
            rows = slice(c * 128, (c + 1) * 128)
            column = to_column(scale[c : c + 1, :])
            raw[rows, COLS:] = (late_raw[rows, :] * column).astype(BF16)
            rest = jnp.broadcast_to(column, (128, 128))
            parts = jnp.zeros((128, 128), F32)
            for i in range(3):
                term = rest.astype(BF16).astype(F32)
                parts = jnp.where(lane == i, term, parts)
                rest = rest - term
            scale_parts[rows, :] = parts.astype(BF16)

    def pack_scales():
        @pl.loop(0, SLOTS // 384)
        def _(i):
            here = pl.ds(pl.multiple_of(i * 384, 384), 384)
            parts = jnp.dot(pack_recv[here, :], scale_parts[...], preferred_element_type=F32)
            columns[here, :] = jnp.sum(parts, axis=1, keepdims=True)

        for d in range(N_SEQ):
            spread = jnp.broadcast_to(columns[d * CAP : (d + 1) * CAP, :], (CAP, 128))
            scale_out[d] = jnp.sum(jnp.where(slots, spread, 0.0), axis=0, keepdims=True)
        scale_in[me] = scale_out[me]

    def scale_arrived():
        for s in range(N_SEQ):
            rows = slice(s * CAP, (s + 1) * CAP)
            spread = jnp.broadcast_to(scale_in[s], (CAP, 128))
            column = jnp.sum(jnp.where(slots, spread, 0.0), axis=1, keepdims=True)
            inbox[R0, rows, :] = (inbox[R0, rows, :].astype(F32) * column).astype(BF16)

    keep_all = jnp.float32(1.0)
    for c in range(GROUPS):
        keep_all = keep_all * keep_of(c)
    keeps[me] = jnp.broadcast_to(keep_all, (1, 128))
    build_pack(send_ref, pack_send)
    staged[0].wait()
    pack_rows(pack_send, k_ref, 0, K0)
    staged[1].wait()
    pack_rows(pack_send, v_ref, 0, V0)
    pl.semaphore_wait(barrier, N_SEQ - 1 + N_HEAD - 1)
    send_rows(lambda peer: keeps.at[me], keeps, 0)
    send_bulk(K0)
    send_bulk(V0)
    build_place(place_send)
    pack_rows(pack_send, k_ref, 1, K1)
    pack_rows(pack_send, v_ref, 1, V1)
    sent_late(K0)
    send_bulk(K1)
    staged[2].wait()
    pack_rows(pack_send, q_ref, 0, Q0)
    pack_rows(pack_send, q_ref, 1, Q1)
    build_pack(receive_ref, pack_recv)
    build_place(place_recv)
    arrived(K0)
    place_rows(place_recv, K0, k_ctx, 0)
    arrived(V0)
    place_rows(place_recv, V0, v_ctx, 0)
    group_states(0)
    send_small(state_out, state_in, 0, st_ssem, st_rsem)
    sent_early(K1)
    send_bulk(V1)
    arrived(K1)
    place_rows(place_recv, K1, k_ctx, 1)
    all_small(state_out, state_in, 0, st_ssem, st_rsem).wait_recv()
    all_rows(keeps, 0).wait_recv()
    prefixes(0)
    send_small(prefix_out, prefix_in, 0, pf_ssem, pf_rsem)
    sent_early(V1)
    send_bulk(Q0)
    arrived(V1)
    place_rows(place_recv, V1, v_ctx, 1)
    group_states(1)
    send_small(state_out, state_in, 1, st_ssem, st_rsem)
    sent_early(Q0)
    send_bulk(Q1)
    all_small(prefix_out, prefix_in, 0, pf_ssem, pf_rsem).wait_recv()
    arrived(Q0)
    place_rows(place_recv, Q0, q_ctx, 0)
    attend(0)
    all_small(state_out, state_in, 1, st_ssem, st_rsem).wait_recv()
    prefixes(1)
    send_small(prefix_out, prefix_in, 1, pf_ssem, pf_rsem)
    pack_rows(pack_recv, raw, 0, R0)
    send_bulk(R0, (0,))
    arrived(Q1)
    place_rows(place_recv, Q1, q_ctx, 1)
    all_small(prefix_out, prefix_in, 1, pf_ssem, pf_rsem).wait_recv()
    attend(1)

    @pl.loop(1, N_HEAD)
    def _(k):
        pltpu.make_async_remote_copy(
            src_ref=z_box.at[mine],
            dst_ref=z_box.at[mine],
            send_sem=z_ssem,
            recv_sem=z_rsem,
            device_id={"seq": me, "head": lax.rem(mine + k, N_HEAD)},
            device_id_type=MESH,
        ).start()

    all_z = pltpu.make_async_remote_copy(
        src_ref=z_box.at[pl.ds(0, N_HEAD - 1)],
        dst_ref=z_box.at[pl.ds(0, N_HEAD - 1)],
        send_sem=z_ssem,
        recv_sem=z_rsem,
        device_id={"seq": me, "head": mine},
        device_id_type=MESH,
    )
    send_bulk(R0, (1,))
    all_z.wait_recv()
    squares = z_box[0]
    for z in range(1, N_HEAD):
        squares = squares + z_box[z]
    normalize(lax.rsqrt(squares / (H * HD) + epsilon))
    pack_scales()
    send_rows(lambda peer: scale_out.at[peer], scale_in, 1)
    pack_rows(pack_recv, raw, 1, R1)
    send_bulk(R1)
    arrived(R0)
    all_rows(scale_in, 1).wait_recv()
    scale_arrived()
    place_rows(place_send, R0, out_ref, 0)
    arrived(R1)
    place_rows(place_send, R1, out_ref, 1)

    all_z.wait_send()
    for stage in (K0, V0, Q1, R0, R1):
        sent_early(stage)
    for stage in (V0, K1, V1, Q0, Q1, R0, R1):
        sent_late(stage)
    for half in range(2):
        all_small(state_out, state_in, half, st_ssem, st_rsem).wait_send()
        all_small(prefix_out, prefix_in, half, pf_ssem, pf_rsem).wait_send()
    all_rows(keeps, 0).wait_send()
    all_rows(scale_in, 1).wait_send()


def shards(query_vectors, key_vectors, value_vectors, send_slots, receive_slots, resets):
    vmem = pl.BlockSpec(memory_space=pltpu.VMEM)
    hbm = pl.BlockSpec(memory_space=pl.ANY)
    square = lambda rows, columns: pltpu.VMEM((rows, columns), BF16)
    row_of_each = lambda: pltpu.VMEM((N_SEQ, 1, 128), F32)
    return pl.pallas_call(
        kernel,
        name="attention",
        out_shape=pltpu.VMEM((TOK, WIDE), BF16),
        in_specs=[hbm, hbm, hbm, vmem, vmem, pl.BlockSpec(memory_space=pltpu.SMEM)],
        out_specs=vmem,
        scratch_shapes=[
            square(TOK, WIDE), square(TOK, WIDE), square(TOK, WIDE), pltpu.VMEM((SLOTS, 1), F32),
            square(SLOTS, TOK), square(TOK, SLOTS), square(SLOTS, TOK), square(TOK, SLOTS),
            pltpu.VMEM((8, SLOTS, COLS), BF16), pltpu.VMEM((8, SLOTS, COLS), BF16),
            square(TOK, WIDE), square(TOK, WIDE), square(TOK, WIDE), square(TOK, WIDE),
            pltpu.VMEM((TOK, COLS), F32),
            pltpu.VMEM((2, GROUPS, COLS, HD), F32), pltpu.VMEM((2, GROUPS, COLS, HD), BF16),
            pltpu.VMEM((2, N_SEQ, PIECE, HD), F32), pltpu.VMEM((2, N_SEQ, PIECE, HD), F32),
            pltpu.VMEM((2, N_SEQ, PIECE, HD), F32), pltpu.VMEM((2, N_SEQ, PIECE, HD), F32),
            row_of_each(), row_of_each(), row_of_each(),
            square(TOK, 128), pltpu.VMEM((TOK // 128, 128), F32), pltpu.VMEM((N_HEAD, TOK // 128, 128), F32),
            pltpu.SemaphoreType.DMA((3,)),
            pltpu.SemaphoreType.DMA((8, 2)), pltpu.SemaphoreType.DMA((8,)),
            pltpu.SemaphoreType.DMA((2,)), pltpu.SemaphoreType.DMA((2,)),
            pltpu.SemaphoreType.DMA((2,)), pltpu.SemaphoreType.DMA((2,)),
            pltpu.SemaphoreType.DMA((2,)), pltpu.SemaphoreType.DMA((2,)),
            pltpu.SemaphoreType.DMA, pltpu.SemaphoreType.DMA,
        ],
        compiler_params=pltpu.CompilerParams(
            collective_id=0, has_side_effects=True, vmem_limit_bytes=60 * 2**20
        ),
    )(query_vectors, key_vectors, value_vectors, send_slots, receive_slots, resets)


def solution(mesh):
    placed = (
        P("seq", "head"),
        P("seq", "head"),
        P("seq", "head"),
        P("seq", None),
        P("seq", None),
        P("seq"),
    )
    return jax.shard_map(shards, mesh=mesh, in_specs=placed, out_specs=P("seq", "head"), check_vma=False)
```

```python
import functools

import jax
import jax.numpy as jnp
from jax import lax
from jax.experimental import pallas as pl
from jax.experimental.pallas import tpu as pltpu
from jax.sharding import PartitionSpec as P

H = 32
HD = 128
CH = 128
CAP = 48
N_SEQ = 32
N_HEAD = 8
TOK = 1024
WIDE = 512
COLS = 256
SLOTS = N_SEQ * CAP
GROUPS = TOK // CH
PIECE = COLS // N_SEQ
EARLY = 16
MESH = pl.DeviceIdType.MESH
BF16 = jnp.bfloat16
F32 = jnp.float32

epsilon = 1e-05

K0, V0, K1, V1, Q0, Q1, R0, R1 = range(8)


def kernel(
    q_hbm, k_hbm, v_hbm, send_ref, receive_ref, resets_ref, out_ref,
    q_ref, k_ref, v_ref, columns,
    pack_send, place_send, pack_recv, place_recv,
    outbox, inbox, q_ctx, k_ctx, v_ctx, raw, kv, carried,
    state_out, state_in, prefix_out, prefix_in, keeps, scale_out, scale_in, scale_parts, partial, z_box,
    in_sem, bulk_ssem, bulk_rsem, st_ssem, st_rsem, pf_ssem, pf_rsem, row_ssem, row_rsem, z_ssem, z_rsem,
):
    me = lax.axis_index("seq")
    mine = lax.axis_index("head")

    barrier = pltpu.get_barrier_semaphore()

    @pl.loop(1, N_SEQ)
    def _(k):
        pl.semaphore_signal(
            barrier, inc=1, device_id={"seq": lax.rem(me + k, N_SEQ), "head": mine}, device_id_type=MESH
        )

    @pl.loop(1, N_HEAD)
    def _(k):
        pl.semaphore_signal(
            barrier, inc=1, device_id={"seq": me, "head": lax.rem(mine + k, N_HEAD)}, device_id_type=MESH
        )

    staged = [
        pltpu.make_async_copy(source, target, in_sem.at[i])
        for i, (source, target) in enumerate([(k_hbm, k_ref), (v_hbm, v_ref), (q_hbm, q_ref)])
    ]
    for copy in staged:
        copy.start()

    diagonal = (
        lax.broadcasted_iota(jnp.int32, (128, 128), 0) == lax.broadcasted_iota(jnp.int32, (128, 128), 1)
    )

    def to_column(row):
        return jnp.sum(jnp.where(diagonal, jnp.broadcast_to(row, (128, 128)), 0.0), axis=1, keepdims=True)

    def to_row(column):
        return jnp.sum(jnp.where(diagonal, jnp.broadcast_to(column, (128, 128)), 0.0), axis=0, keepdims=True)

    def build_pack(table_ref, pack):
        corner = diagonal[:CAP, :CAP]
        for d in range(N_SEQ):
            row = jnp.broadcast_to(table_ref[d : d + 1, :].astype(F32), (CAP, CAP))
            column = jnp.sum(jnp.where(corner, row, 0.0), axis=1, keepdims=True)
            spots = lax.broadcasted_iota(jnp.int32, (CAP, TOK), 1).astype(F32)
            pack[d * CAP : (d + 1) * CAP, :] = jnp.where(spots == column, 1.0, 0.0).astype(BF16)
            columns[d * CAP : (d + 1) * CAP, :] = column

    def build_place(place):
        for i in range(SLOTS // 128):
            row = to_row(columns[i * 128 : (i + 1) * 128, :])

            @pl.loop(0, TOK // 256)
            def _(j):
                spots = (lax.broadcasted_iota(jnp.int32, (256, 128), 0) + j * 256).astype(F32)
                place[pl.ds(pl.multiple_of(j * 256, 256), 256), i * 128 : (i + 1) * 128] = jnp.where(
                    spots == row, 1.0, 0.0
                ).astype(BF16)

    def pack_rows(pack, rows_ref, half, stage):
        @pl.loop(0, SLOTS // 384)
        def _(i):
            here = pl.ds(pl.multiple_of(i * 384, 384), 384)
            outbox[stage, here, :] = jnp.dot(
                pack[here, :], rows_ref[:, half * COLS : (half + 1) * COLS], preferred_element_type=F32
            ).astype(BF16)

    def place_rows(place, stage, rows_ref, half):
        @pl.loop(0, TOK // 256)
        def _(i):
            here = pl.ds(pl.multiple_of(i * 256, 256), 256)
            rows_ref[here, half * COLS : (half + 1) * COLS] = jnp.dot(
                place[here, :], inbox[stage], preferred_element_type=F32
            ).astype(BF16)

    def block(device):
        return pl.ds(pl.multiple_of(device * CAP, CAP), CAP)

    def send_bulk(stage, parts=(0, 1)):
        def send(part):
            def one(k):
                peer = lax.rem(me + 13 * k, N_SEQ)
                pltpu.make_async_remote_copy(
                    src_ref=outbox.at[stage, block(peer), :],
                    dst_ref=inbox.at[stage, block(me), :],
                    send_sem=bulk_ssem.at[stage, part],
                    recv_sem=bulk_rsem.at[stage],
                    device_id={"seq": peer, "head": mine},
                    device_id_type=MESH,
                ).start()

            return one

        if 0 in parts:
            pl.loop(1, EARLY + 1)(send(0))
            inbox[stage, block(me), :] = outbox[stage, block(me), :]
        if 1 in parts:
            pl.loop(EARLY + 1, N_SEQ)(send(1))

    def bulk_of(stage, blocks, part):
        rows = pl.ds(0, blocks * CAP)
        return pltpu.make_async_remote_copy(
            src_ref=outbox.at[stage, rows, :],
            dst_ref=inbox.at[stage, rows, :],
            send_sem=bulk_ssem.at[stage, part],
            recv_sem=bulk_rsem.at[stage],
            device_id={"seq": me, "head": mine},
            device_id_type=MESH,
        )

    def arrived(stage):
        bulk_of(stage, N_SEQ - 1, 0).wait_recv()

    def sent_early(stage):
        bulk_of(stage, EARLY, 0).wait_send()

    def sent_late(stage):
        bulk_of(stage, N_SEQ - 1 - EARLY, 1).wait_send()

    def send_small(source, target, half, ssem, rsem):
        @pl.loop(1, N_SEQ)
        def _(k):
            peer = lax.rem(me + 13 * k, N_SEQ)
            pltpu.make_async_remote_copy(
                src_ref=source.at[half, peer],
                dst_ref=target.at[half, me],
                send_sem=ssem.at[half],
                recv_sem=rsem.at[half],
                device_id={"seq": peer, "head": mine},
                device_id_type=MESH,
            ).start()

        target[half, me] = source[half, me]

    def all_small(source, target, half, ssem, rsem):
        return pltpu.make_async_remote_copy(
            src_ref=source.at[half, pl.ds(0, N_SEQ - 1)],
            dst_ref=target.at[half, pl.ds(0, N_SEQ - 1)],
            send_sem=ssem.at[half],
            recv_sem=rsem.at[half],
            device_id={"seq": me, "head": mine},
            device_id_type=MESH,
        )

    def send_rows(source_of, target, which):
        @pl.loop(1, N_SEQ)
        def _(k):
            peer = lax.rem(me + 13 * k, N_SEQ)
            pltpu.make_async_remote_copy(
                src_ref=source_of(peer),
                dst_ref=target.at[me],
                send_sem=row_ssem.at[which],
                recv_sem=row_rsem.at[which],
                device_id={"seq": peer, "head": mine},
                device_id_type=MESH,
            ).start()

    def all_rows(target, which):
        most = pl.ds(0, N_SEQ - 1)
        return pltpu.make_async_remote_copy(
            src_ref=target.at[most],
            dst_ref=target.at[most],
            send_sem=row_ssem.at[which],
            recv_sem=row_rsem.at[which],
            device_id={"seq": me, "head": mine},
            device_id_type=MESH,
        )

    def keep_of(group):
        return 1.0 - resets_ref[group].astype(F32)

    def group_states(half):
        state = [jnp.zeros((HD, HD), F32), jnp.zeros((HD, HD), F32)]
        for c in range(GROUPS):
            keep = keep_of(c)
            for h in range(2):
                cols = slice(half * COLS + h * HD, half * COLS + (h + 1) * HD)
                rows = slice(c * CH, (c + 1) * CH)
                group_kv = lax.dot_general(
                    k_ctx[rows, cols], v_ctx[rows, cols], (((0,), (0,)), ((), ())), preferred_element_type=F32
                )
                kv[half, c, h * HD : (h + 1) * HD, :] = group_kv
                state[h] = state[h] * keep + group_kv
        for h in range(2):
            state_out[half, h * 16 : (h + 1) * 16] = state[h].reshape(16, PIECE, HD)

    def prefixes(half):
        total = jnp.zeros((PIECE, HD), F32)
        for s in range(N_SEQ):
            prefix_out[half, s] = total
            total = state_in[half, s] + keeps[s] * total

    def attend(half):
        causal = (
            lax.broadcasted_iota(jnp.int32, (CH, CH), 0) >= lax.broadcasted_iota(jnp.int32, (CH, CH), 1)
        )
        for h in range(2):
            state = prefix_in[half, h * 16 : (h + 1) * 16].reshape(HD, HD)
            for c in range(GROUPS):
                state = state * keep_of(c)
                carried[half, c, h * HD : (h + 1) * HD, :] = state.astype(BF16)
                state = state + kv[half, c, h * HD : (h + 1) * HD, :]
        for c in range(GROUPS):
            rows = slice(c * CH, (c + 1) * CH)
            squares = jnp.zeros((CH, HD), F32)
            for h in range(2):
                cols = slice(half * COLS + h * HD, half * COLS + (h + 1) * HD)
                q = q_ctx[rows, cols]
                scores = lax.dot_general(
                    q, k_ctx[rows, cols], (((1,), (1,)), ((), ())), preferred_element_type=F32
                )
                weights = jnp.where(causal, scores, 0.0).astype(BF16)
                value = jnp.dot(q, carried[half, c, h * HD : (h + 1) * HD, :], preferred_element_type=F32)
                value = value + jnp.dot(weights, v_ctx[rows, cols], preferred_element_type=F32)
                squares = squares + value * value
                raw[rows, cols] = value.astype(BF16)
            row = to_row(jnp.sum(squares, axis=1, keepdims=True))
            if half == 0:
                partial[c : c + 1, :] = row
            else:
                z_box[mine, c : c + 1, :] = partial[c : c + 1, :] + row

    slots = (
        lax.broadcasted_iota(jnp.int32, (CAP, 128), 0) == lax.broadcasted_iota(jnp.int32, (CAP, 128), 1)
    )

    def split_scale(scale):
        lane = lax.broadcasted_iota(jnp.int32, (128, 128), 1)
        for c in range(TOK // 128):
            rows = slice(c * 128, (c + 1) * 128)
            column = to_column(scale[c : c + 1, :])
            rest = jnp.broadcast_to(column, (128, 128))
            parts = jnp.zeros((128, 128), F32)
            for i in range(3):
                term = rest.astype(BF16).astype(F32)
                parts = jnp.where(lane == i, term, parts)
                rest = rest - term
            scale_parts[rows, :] = parts.astype(BF16)

    def pack_scales():
        @pl.loop(0, SLOTS // 384)
        def _(i):
            here = pl.ds(pl.multiple_of(i * 384, 384), 384)
            parts = jnp.dot(pack_recv[here, :], scale_parts[...], preferred_element_type=F32)
            columns[here, :] = jnp.sum(parts, axis=1, keepdims=True)

        for d in range(N_SEQ):
            spread = jnp.broadcast_to(columns[d * CAP : (d + 1) * CAP, :], (CAP, 128))
            scale_out[d] = jnp.sum(jnp.where(slots, spread, 0.0), axis=0, keepdims=True)
        scale_in[me] = scale_out[me]

    def scales_to_columns():
        for d in range(N_SEQ):
            spread = jnp.broadcast_to(scale_in[d], (CAP, 128))
            columns[d * CAP : (d + 1) * CAP, :] = jnp.sum(jnp.where(slots, spread, 0.0), axis=1, keepdims=True)

    def scale_rows(stage):
        @pl.loop(0, SLOTS // 384)
        def _(i):
            here = pl.ds(pl.multiple_of(i * 384, 384), 384)
            inbox[stage, here, :] = (inbox[stage, here, :].astype(F32) * columns[here, :]).astype(BF16)

    keep_all = jnp.float32(1.0)
    for c in range(GROUPS):
        keep_all = keep_all * keep_of(c)
    keeps[me] = jnp.broadcast_to(keep_all, (1, 128))
    build_pack(send_ref, pack_send)
    staged[0].wait()
    pack_rows(pack_send, k_ref, 0, K0)
    staged[1].wait()
    pack_rows(pack_send, v_ref, 0, V0)
    pl.semaphore_wait(barrier, N_SEQ - 1 + N_HEAD - 1)
    send_rows(lambda peer: keeps.at[me], keeps, 0)
    send_bulk(K0)
    send_bulk(V0)
    build_place(place_send)
    pack_rows(pack_send, k_ref, 1, K1)
    pack_rows(pack_send, v_ref, 1, V1)
    sent_late(K0)
    send_bulk(K1)
    staged[2].wait()
    pack_rows(pack_send, q_ref, 0, Q0)
    pack_rows(pack_send, q_ref, 1, Q1)
    build_pack(receive_ref, pack_recv)
    build_place(place_recv)
    arrived(K0)
    place_rows(place_recv, K0, k_ctx, 0)
    arrived(V0)
    place_rows(place_recv, V0, v_ctx, 0)
    group_states(0)
    send_small(state_out, state_in, 0, st_ssem, st_rsem)
    sent_early(K1)
    send_bulk(V1)
    arrived(K1)
    place_rows(place_recv, K1, k_ctx, 1)
    all_small(state_out, state_in, 0, st_ssem, st_rsem).wait_recv()
    all_rows(keeps, 0).wait_recv()
    prefixes(0)
    send_small(prefix_out, prefix_in, 0, pf_ssem, pf_rsem)
    sent_early(V1)
    send_bulk(Q0)
    arrived(V1)
    place_rows(place_recv, V1, v_ctx, 1)
    group_states(1)
    send_small(state_out, state_in, 1, st_ssem, st_rsem)
    sent_early(Q0)
    send_bulk(Q1)
    all_small(prefix_out, prefix_in, 0, pf_ssem, pf_rsem).wait_recv()
    arrived(Q0)
    place_rows(place_recv, Q0, q_ctx, 0)
    attend(0)
    all_small(state_out, state_in, 1, st_ssem, st_rsem).wait_recv()
    prefixes(1)
    send_small(prefix_out, prefix_in, 1, pf_ssem, pf_rsem)
    pack_rows(pack_recv, raw, 0, R0)
    send_bulk(R0, (0,))
    arrived(Q1)
    place_rows(place_recv, Q1, q_ctx, 1)
    all_small(prefix_out, prefix_in, 1, pf_ssem, pf_rsem).wait_recv()
    attend(1)

    @pl.loop(1, N_HEAD)
    def _(k):
        pltpu.make_async_remote_copy(
            src_ref=z_box.at[mine],
            dst_ref=z_box.at[mine],
            send_sem=z_ssem,
            recv_sem=z_rsem,
            device_id={"seq": me, "head": lax.rem(mine + k, N_HEAD)},
            device_id_type=MESH,
        ).start()

    all_z = pltpu.make_async_remote_copy(
        src_ref=z_box.at[pl.ds(0, N_HEAD - 1)],
        dst_ref=z_box.at[pl.ds(0, N_HEAD - 1)],
        send_sem=z_ssem,
        recv_sem=z_rsem,
        device_id={"seq": me, "head": mine},
        device_id_type=MESH,
    )
    send_bulk(R0, (1,))
    pack_rows(pack_recv, raw, 1, R1)
    send_bulk(R1, (0,))
    all_z.wait_recv()
    squares = z_box[0]
    for z in range(1, N_HEAD):
        squares = squares + z_box[z]
    split_scale(lax.rsqrt(squares / (H * HD) + epsilon))
    pack_scales()
    send_rows(lambda peer: scale_out.at[peer], scale_in, 1)
    send_bulk(R1, (1,))
    arrived(R0)
    all_rows(scale_in, 1).wait_recv()
    scales_to_columns()
    scale_rows(R0)
    place_rows(place_send, R0, out_ref, 0)
    arrived(R1)
    scale_rows(R1)
    place_rows(place_send, R1, out_ref, 1)

    all_z.wait_send()
    for stage in (K0, V0, Q1, R0, R1):
        sent_early(stage)
    for stage in (V0, K1, V1, Q0, Q1, R0, R1):
        sent_late(stage)
    for half in range(2):
        all_small(state_out, state_in, half, st_ssem, st_rsem).wait_send()
        all_small(prefix_out, prefix_in, half, pf_ssem, pf_rsem).wait_send()
    all_rows(keeps, 0).wait_send()
    all_rows(scale_in, 1).wait_send()


def shards(query_vectors, key_vectors, value_vectors, send_slots, receive_slots, resets):
    vmem = pl.BlockSpec(memory_space=pltpu.VMEM)
    hbm = pl.BlockSpec(memory_space=pl.ANY)
    square = lambda rows, columns: pltpu.VMEM((rows, columns), BF16)
    row_of_each = lambda: pltpu.VMEM((N_SEQ, 1, 128), F32)
    return pl.pallas_call(
        kernel,
        name="attention",
        out_shape=pltpu.VMEM((TOK, WIDE), BF16),
        in_specs=[hbm, hbm, hbm, vmem, vmem, pl.BlockSpec(memory_space=pltpu.SMEM)],
        out_specs=vmem,
        scratch_shapes=[
            square(TOK, WIDE), square(TOK, WIDE), square(TOK, WIDE), pltpu.VMEM((SLOTS, 1), F32),
            square(SLOTS, TOK), square(TOK, SLOTS), square(SLOTS, TOK), square(TOK, SLOTS),
            pltpu.VMEM((8, SLOTS, COLS), BF16), pltpu.VMEM((8, SLOTS, COLS), BF16),
            square(TOK, WIDE), square(TOK, WIDE), square(TOK, WIDE), square(TOK, WIDE),
            pltpu.VMEM((2, GROUPS, COLS, HD), F32), pltpu.VMEM((2, GROUPS, COLS, HD), BF16),
            pltpu.VMEM((2, N_SEQ, PIECE, HD), F32), pltpu.VMEM((2, N_SEQ, PIECE, HD), F32),
            pltpu.VMEM((2, N_SEQ, PIECE, HD), F32), pltpu.VMEM((2, N_SEQ, PIECE, HD), F32),
            row_of_each(), row_of_each(), row_of_each(),
            square(TOK, 128), pltpu.VMEM((TOK // 128, 128), F32), pltpu.VMEM((N_HEAD, TOK // 128, 128), F32),
            pltpu.SemaphoreType.DMA((3,)),
            pltpu.SemaphoreType.DMA((8, 2)), pltpu.SemaphoreType.DMA((8,)),
            pltpu.SemaphoreType.DMA((2,)), pltpu.SemaphoreType.DMA((2,)),
            pltpu.SemaphoreType.DMA((2,)), pltpu.SemaphoreType.DMA((2,)),
            pltpu.SemaphoreType.DMA((2,)), pltpu.SemaphoreType.DMA((2,)),
            pltpu.SemaphoreType.DMA, pltpu.SemaphoreType.DMA,
        ],
        compiler_params=pltpu.CompilerParams(
            collective_id=0, has_side_effects=True, vmem_limit_bytes=60 * 2**20
        ),
    )(query_vectors, key_vectors, value_vectors, send_slots, receive_slots, resets)


def solution(mesh):
    placed = (
        P("seq", "head"),
        P("seq", "head"),
        P("seq", "head"),
        P("seq", None),
        P("seq", None),
        P("seq"),
    )
    return jax.shard_map(shards, mesh=mesh, in_specs=placed, out_specs=P("seq", "head"), check_vma=False)
```

```python
import functools

import jax
import jax.numpy as jnp
from jax import lax
from jax.experimental import pallas as pl
from jax.experimental.pallas import tpu as pltpu
from jax.sharding import PartitionSpec as P

H = 32
HD = 128
CH = 128
CAP = 48
N_SEQ = 32
N_HEAD = 8
TOK = 1024
WIDE = 512
COLS = 256
SLOTS = N_SEQ * CAP
GROUPS = TOK // CH
PIECE = COLS // N_SEQ
EARLY = 16
MESH = pl.DeviceIdType.MESH
BF16 = jnp.bfloat16
F32 = jnp.float32

epsilon = 1e-05

K0, V0, K1, V1, Q0, Q1, R0, R1 = range(8)


def kernel(
    q_hbm, k_hbm, v_hbm, send_ref, receive_ref, resets_ref, out_ref,
    q_ref, k_ref, v_ref, columns,
    pack_send, place_send, pack_recv, place_recv,
    outbox, inbox, q_ctx, k_ctx, v_ctx, raw, kv, carried,
    state_out, state_in, prefix_out, prefix_in, keeps, scale_out, scale_in, scale_parts, slot_parts, partial, z_box,
    in_sem, bulk_ssem, bulk_rsem, st_ssem, st_rsem, pf_ssem, pf_rsem, row_ssem, row_rsem, z_ssem, z_rsem,
):
    me = lax.axis_index("seq")
    mine = lax.axis_index("head")

    barrier = pltpu.get_barrier_semaphore()

    @pl.loop(1, N_SEQ)
    def _(k):
        pl.semaphore_signal(
            barrier, inc=1, device_id={"seq": lax.rem(me + k, N_SEQ), "head": mine}, device_id_type=MESH
        )

    @pl.loop(1, N_HEAD)
    def _(k):
        pl.semaphore_signal(
            barrier, inc=1, device_id={"seq": me, "head": lax.rem(mine + k, N_HEAD)}, device_id_type=MESH
        )

    staged = [
        pltpu.make_async_copy(source, target, in_sem.at[i])
        for i, (source, target) in enumerate([(k_hbm, k_ref), (v_hbm, v_ref), (q_hbm, q_ref)])
    ]
    for copy in staged:
        copy.start()

    diagonal = (
        lax.broadcasted_iota(jnp.int32, (128, 128), 0) == lax.broadcasted_iota(jnp.int32, (128, 128), 1)
    )

    def to_column(row):
        return jnp.sum(jnp.where(diagonal, jnp.broadcast_to(row, (128, 128)), 0.0), axis=1, keepdims=True)

    def to_row(column):
        return jnp.sum(jnp.where(diagonal, jnp.broadcast_to(column, (128, 128)), 0.0), axis=0, keepdims=True)

    def build_pack(table_ref, pack):
        corner = diagonal[:CAP, :CAP]
        for d in range(N_SEQ):
            row = jnp.broadcast_to(table_ref[d : d + 1, :].astype(F32), (CAP, CAP))
            column = jnp.sum(jnp.where(corner, row, 0.0), axis=1, keepdims=True)
            spots = lax.broadcasted_iota(jnp.int32, (CAP, TOK), 1).astype(F32)
            pack[d * CAP : (d + 1) * CAP, :] = jnp.where(spots == column, 1.0, 0.0).astype(BF16)
            columns[d * CAP : (d + 1) * CAP, :] = column

    def build_place(place):
        for i in range(SLOTS // 128):
            row = to_row(columns[i * 128 : (i + 1) * 128, :])

            @pl.loop(0, TOK // 256)
            def _(j):
                spots = (lax.broadcasted_iota(jnp.int32, (256, 128), 0) + j * 256).astype(F32)
                place[pl.ds(pl.multiple_of(j * 256, 256), 256), i * 128 : (i + 1) * 128] = jnp.where(
                    spots == row, 1.0, 0.0
                ).astype(BF16)

    def pack_rows(pack, rows_ref, half, stage):
        @pl.loop(0, SLOTS // 384)
        def _(i):
            here = pl.ds(pl.multiple_of(i * 384, 384), 384)
            outbox[stage, here, :] = jnp.dot(
                pack[here, :], rows_ref[:, half * COLS : (half + 1) * COLS], preferred_element_type=F32
            ).astype(BF16)

    def place_rows(place, stage, rows_ref, half):
        @pl.loop(0, TOK // 256)
        def _(i):
            here = pl.ds(pl.multiple_of(i * 256, 256), 256)
            rows_ref[here, half * COLS : (half + 1) * COLS] = jnp.dot(
                place[here, :], inbox[stage], preferred_element_type=F32
            ).astype(BF16)

    def block(device):
        return pl.ds(pl.multiple_of(device * CAP, CAP), CAP)

    def send_bulk(stage, parts=(0, 1)):
        def send(part):
            def one(k):
                peer = lax.rem(me + 13 * k, N_SEQ)
                pltpu.make_async_remote_copy(
                    src_ref=outbox.at[stage, block(peer), :],
                    dst_ref=inbox.at[stage, block(me), :],
                    send_sem=bulk_ssem.at[stage, part],
                    recv_sem=bulk_rsem.at[stage],
                    device_id={"seq": peer, "head": mine},
                    device_id_type=MESH,
                ).start()

            return one

        if 0 in parts:
            pl.loop(1, EARLY + 1)(send(0))
            inbox[stage, block(me), :] = outbox[stage, block(me), :]
        if 1 in parts:
            pl.loop(EARLY + 1, N_SEQ)(send(1))

    def bulk_of(stage, blocks, part):
        rows = pl.ds(0, blocks * CAP)
        return pltpu.make_async_remote_copy(
            src_ref=outbox.at[stage, rows, :],
            dst_ref=inbox.at[stage, rows, :],
            send_sem=bulk_ssem.at[stage, part],
            recv_sem=bulk_rsem.at[stage],
            device_id={"seq": me, "head": mine},
            device_id_type=MESH,
        )

    def arrived(stage):
        bulk_of(stage, N_SEQ - 1, 0).wait_recv()

    def sent_early(stage):
        bulk_of(stage, EARLY, 0).wait_send()

    def sent_late(stage):
        bulk_of(stage, N_SEQ - 1 - EARLY, 1).wait_send()

    def send_small(source, target, half, ssem, rsem):
        @pl.loop(1, N_SEQ)
        def _(k):
            peer = lax.rem(me + 13 * k, N_SEQ)
            pltpu.make_async_remote_copy(
                src_ref=source.at[half, peer],
                dst_ref=target.at[half, me],
                send_sem=ssem.at[half],
                recv_sem=rsem.at[half],
                device_id={"seq": peer, "head": mine},
                device_id_type=MESH,
            ).start()

        target[half, me] = source[half, me]

    def all_small(source, target, half, ssem, rsem):
        return pltpu.make_async_remote_copy(
            src_ref=source.at[half, pl.ds(0, N_SEQ - 1)],
            dst_ref=target.at[half, pl.ds(0, N_SEQ - 1)],
            send_sem=ssem.at[half],
            recv_sem=rsem.at[half],
            device_id={"seq": me, "head": mine},
            device_id_type=MESH,
        )

    def send_rows(source_of, target, which):
        @pl.loop(1, N_SEQ)
        def _(k):
            peer = lax.rem(me + 13 * k, N_SEQ)
            pltpu.make_async_remote_copy(
                src_ref=source_of(peer),
                dst_ref=target.at[me],
                send_sem=row_ssem.at[which],
                recv_sem=row_rsem.at[which],
                device_id={"seq": peer, "head": mine},
                device_id_type=MESH,
            ).start()

    def all_rows(target, which):
        most = pl.ds(0, N_SEQ - 1)
        return pltpu.make_async_remote_copy(
            src_ref=target.at[most],
            dst_ref=target.at[most],
            send_sem=row_ssem.at[which],
            recv_sem=row_rsem.at[which],
            device_id={"seq": me, "head": mine},
            device_id_type=MESH,
        )

    def keep_of(group):
        return 1.0 - resets_ref[group].astype(F32)

    def group_states(half):
        state = [jnp.zeros((HD, HD), F32), jnp.zeros((HD, HD), F32)]
        for c in range(GROUPS):
            keep = keep_of(c)
            for h in range(2):
                cols = slice(half * COLS + h * HD, half * COLS + (h + 1) * HD)
                rows = slice(c * CH, (c + 1) * CH)
                group_kv = lax.dot_general(
                    k_ctx[rows, cols], v_ctx[rows, cols], (((0,), (0,)), ((), ())), preferred_element_type=F32
                )
                kv[half, c, h * HD : (h + 1) * HD, :] = group_kv
                state[h] = state[h] * keep + group_kv
        for h in range(2):
            state_out[half, h * 16 : (h + 1) * 16] = state[h].reshape(16, PIECE, HD)

    def prefixes(half):
        total = jnp.zeros((PIECE, HD), F32)
        for s in range(N_SEQ):
            prefix_out[half, s] = total
            total = state_in[half, s] + keeps[s] * total

    def attend(half):
        causal = (
            lax.broadcasted_iota(jnp.int32, (CH, CH), 0) >= lax.broadcasted_iota(jnp.int32, (CH, CH), 1)
        )
        for h in range(2):
            state = prefix_in[half, h * 16 : (h + 1) * 16].reshape(HD, HD)
            for c in range(GROUPS):
                state = state * keep_of(c)
                carried[half, c, h * HD : (h + 1) * HD, :] = state.astype(BF16)
                state = state + kv[half, c, h * HD : (h + 1) * HD, :]
        for c in range(GROUPS):
            rows = slice(c * CH, (c + 1) * CH)
            squares = jnp.zeros((CH, HD), F32)
            for h in range(2):
                cols = slice(half * COLS + h * HD, half * COLS + (h + 1) * HD)
                q = q_ctx[rows, cols]
                scores = lax.dot_general(
                    q, k_ctx[rows, cols], (((1,), (1,)), ((), ())), preferred_element_type=F32
                )
                weights = jnp.where(causal, scores, 0.0).astype(BF16)
                value = jnp.dot(q, carried[half, c, h * HD : (h + 1) * HD, :], preferred_element_type=F32)
                value = value + jnp.dot(weights, v_ctx[rows, cols], preferred_element_type=F32)
                squares = squares + value * value
                raw[rows, cols] = value.astype(BF16)
            row = to_row(jnp.sum(squares, axis=1, keepdims=True))
            if half == 0:
                partial[c : c + 1, :] = row
            else:
                z_box[mine, c : c + 1, :] = partial[c : c + 1, :] + row

    slots = (
        lax.broadcasted_iota(jnp.int32, (CAP, 128), 0) == lax.broadcasted_iota(jnp.int32, (CAP, 128), 1)
    )

    def three_terms(column, rows):
        lane = lax.broadcasted_iota(jnp.int32, (rows, 128), 1)
        rest = jnp.broadcast_to(column, (rows, 128))
        parts = jnp.zeros((rows, 128), F32)
        for i in range(3):
            term = rest.astype(BF16).astype(F32)
            parts = jnp.where(lane == i, term, parts)
            rest = rest - term
        return parts.astype(BF16)

    def split_scale(scale):
        for c in range(TOK // 128):
            scale_parts[c * 128 : (c + 1) * 128, :] = three_terms(to_column(scale[c : c + 1, :]), 128)

    def pack_scales():
        @pl.loop(0, SLOTS // 384)
        def _(i):
            here = pl.ds(pl.multiple_of(i * 384, 384), 384)
            parts = jnp.dot(pack_recv[here, :], scale_parts[...], preferred_element_type=F32)
            columns[here, :] = jnp.sum(parts, axis=1, keepdims=True)

        for d in range(N_SEQ):
            spread = jnp.broadcast_to(columns[d * CAP : (d + 1) * CAP, :], (CAP, 128))
            scale_out[d] = jnp.sum(jnp.where(slots, spread, 0.0), axis=0, keepdims=True)
        scale_in[me] = scale_out[me]

    def place_scales():
        for d in range(N_SEQ):
            spread = jnp.broadcast_to(scale_in[d], (CAP, 128))
            column = jnp.sum(jnp.where(slots, spread, 0.0), axis=1, keepdims=True)
            slot_parts[d * CAP : (d + 1) * CAP, :] = three_terms(column, CAP)

        @pl.loop(0, TOK // 256)
        def _(i):
            here = pl.ds(pl.multiple_of(i * 256, 256), 256)
            parts = jnp.dot(place_send[here, :], slot_parts[...], preferred_element_type=F32)
            columns[here, :] = jnp.sum(parts, axis=1, keepdims=True)

    def place_scaled(stage, half):
        @pl.loop(0, TOK // 256)
        def _(i):
            here = pl.ds(pl.multiple_of(i * 256, 256), 256)
            rows = jnp.dot(place_send[here, :], inbox[stage], preferred_element_type=F32)
            out_ref[here, half * COLS : (half + 1) * COLS] = (rows * columns[here, :]).astype(BF16)

    keep_all = jnp.float32(1.0)
    for c in range(GROUPS):
        keep_all = keep_all * keep_of(c)
    keeps[me] = jnp.broadcast_to(keep_all, (1, 128))
    build_pack(send_ref, pack_send)
    staged[0].wait()
    pack_rows(pack_send, k_ref, 0, K0)
    staged[1].wait()
    pack_rows(pack_send, v_ref, 0, V0)
    pl.semaphore_wait(barrier, N_SEQ - 1 + N_HEAD - 1)
    send_rows(lambda peer: keeps.at[me], keeps, 0)
    send_bulk(K0)
    send_bulk(V0)
    build_place(place_send)
    pack_rows(pack_send, k_ref, 1, K1)
    pack_rows(pack_send, v_ref, 1, V1)
    sent_late(K0)
    send_bulk(K1)
    staged[2].wait()
    pack_rows(pack_send, q_ref, 0, Q0)
    pack_rows(pack_send, q_ref, 1, Q1)
    build_pack(receive_ref, pack_recv)
    build_place(place_recv)
    arrived(K0)
    place_rows(place_recv, K0, k_ctx, 0)
    arrived(V0)
    place_rows(place_recv, V0, v_ctx, 0)
    group_states(0)
    send_small(state_out, state_in, 0, st_ssem, st_rsem)
    sent_early(K1)
    send_bulk(V1)
    arrived(K1)
    place_rows(place_recv, K1, k_ctx, 1)
    all_small(state_out, state_in, 0, st_ssem, st_rsem).wait_recv()
    all_rows(keeps, 0).wait_recv()
    prefixes(0)
    send_small(prefix_out, prefix_in, 0, pf_ssem, pf_rsem)
    sent_early(V1)
    send_bulk(Q0)
    arrived(V1)
    place_rows(place_recv, V1, v_ctx, 1)
    group_states(1)
    send_small(state_out, state_in, 1, st_ssem, st_rsem)
    sent_early(Q0)
    send_bulk(Q1)
    all_small(prefix_out, prefix_in, 0, pf_ssem, pf_rsem).wait_recv()
    arrived(Q0)
    place_rows(place_recv, Q0, q_ctx, 0)
    attend(0)
    all_small(state_out, state_in, 1, st_ssem, st_rsem).wait_recv()
    prefixes(1)
    send_small(prefix_out, prefix_in, 1, pf_ssem, pf_rsem)
    pack_rows(pack_recv, raw, 0, R0)
    send_bulk(R0, (0,))
    arrived(Q1)
    place_rows(place_recv, Q1, q_ctx, 1)
    all_small(prefix_out, prefix_in, 1, pf_ssem, pf_rsem).wait_recv()
    attend(1)

    @pl.loop(1, N_HEAD)
    def _(k):
        pltpu.make_async_remote_copy(
            src_ref=z_box.at[mine],
            dst_ref=z_box.at[mine],
            send_sem=z_ssem,
            recv_sem=z_rsem,
            device_id={"seq": me, "head": lax.rem(mine + k, N_HEAD)},
            device_id_type=MESH,
        ).start()

    all_z = pltpu.make_async_remote_copy(
        src_ref=z_box.at[pl.ds(0, N_HEAD - 1)],
        dst_ref=z_box.at[pl.ds(0, N_HEAD - 1)],
        send_sem=z_ssem,
        recv_sem=z_rsem,
        device_id={"seq": me, "head": mine},
        device_id_type=MESH,
    )
    send_bulk(R0, (1,))
    pack_rows(pack_recv, raw, 1, R1)
    send_bulk(R1, (0,))
    all_z.wait_recv()
    squares = z_box[0]
    for z in range(1, N_HEAD):
        squares = squares + z_box[z]
    split_scale(lax.rsqrt(squares / (H * HD) + epsilon))
    pack_scales()
    send_rows(lambda peer: scale_out.at[peer], scale_in, 1)
    send_bulk(R1, (1,))
    arrived(R0)
    all_rows(scale_in, 1).wait_recv()
    place_scales()
    place_scaled(R0, 0)
    arrived(R1)
    place_scaled(R1, 1)

    all_z.wait_send()
    for stage in (K0, V0, Q1, R0, R1):
        sent_early(stage)
    for stage in (V0, K1, V1, Q0, Q1, R0, R1):
        sent_late(stage)
    for half in range(2):
        all_small(state_out, state_in, half, st_ssem, st_rsem).wait_send()
        all_small(prefix_out, prefix_in, half, pf_ssem, pf_rsem).wait_send()
    all_rows(keeps, 0).wait_send()
    all_rows(scale_in, 1).wait_send()


def shards(query_vectors, key_vectors, value_vectors, send_slots, receive_slots, resets):
    vmem = pl.BlockSpec(memory_space=pltpu.VMEM)
    hbm = pl.BlockSpec(memory_space=pl.ANY)
    square = lambda rows, columns: pltpu.VMEM((rows, columns), BF16)
    row_of_each = lambda: pltpu.VMEM((N_SEQ, 1, 128), F32)
    return pl.pallas_call(
        kernel,
        name="attention",
        out_shape=pltpu.VMEM((TOK, WIDE), BF16),
        in_specs=[hbm, hbm, hbm, vmem, vmem, pl.BlockSpec(memory_space=pltpu.SMEM)],
        out_specs=vmem,
        scratch_shapes=[
            square(TOK, WIDE), square(TOK, WIDE), square(TOK, WIDE), pltpu.VMEM((SLOTS, 1), F32),
            square(SLOTS, TOK), square(TOK, SLOTS), square(SLOTS, TOK), square(TOK, SLOTS),
            pltpu.VMEM((8, SLOTS, COLS), BF16), pltpu.VMEM((8, SLOTS, COLS), BF16),
            square(TOK, WIDE), square(TOK, WIDE), square(TOK, WIDE), square(TOK, WIDE),
            pltpu.VMEM((2, GROUPS, COLS, HD), F32), pltpu.VMEM((2, GROUPS, COLS, HD), BF16),
            pltpu.VMEM((2, N_SEQ, PIECE, HD), F32), pltpu.VMEM((2, N_SEQ, PIECE, HD), F32),
            pltpu.VMEM((2, N_SEQ, PIECE, HD), F32), pltpu.VMEM((2, N_SEQ, PIECE, HD), F32),
            row_of_each(), row_of_each(), row_of_each(),
            square(TOK, 128), square(SLOTS, 128), pltpu.VMEM((TOK // 128, 128), F32), pltpu.VMEM((N_HEAD, TOK // 128, 128), F32),
            pltpu.SemaphoreType.DMA((3,)),
            pltpu.SemaphoreType.DMA((8, 2)), pltpu.SemaphoreType.DMA((8,)),
            pltpu.SemaphoreType.DMA((2,)), pltpu.SemaphoreType.DMA((2,)),
            pltpu.SemaphoreType.DMA((2,)), pltpu.SemaphoreType.DMA((2,)),
            pltpu.SemaphoreType.DMA((2,)), pltpu.SemaphoreType.DMA((2,)),
            pltpu.SemaphoreType.DMA, pltpu.SemaphoreType.DMA,
        ],
        compiler_params=pltpu.CompilerParams(
            collective_id=0, has_side_effects=True, vmem_limit_bytes=60 * 2**20
        ),
    )(query_vectors, key_vectors, value_vectors, send_slots, receive_slots, resets)


def solution(mesh):
    placed = (
        P("seq", "head"),
        P("seq", "head"),
        P("seq", "head"),
        P("seq", None),
        P("seq", None),
        P("seq"),
    )
    return jax.shard_map(shards, mesh=mesh, in_specs=placed, out_specs=P("seq", "head"), check_vma=False)
```

```python
import functools

import jax
import jax.numpy as jnp
from jax import lax
from jax.experimental import pallas as pl
from jax.experimental.pallas import tpu as pltpu
from jax.sharding import PartitionSpec as P

H = 32
HD = 128
CH = 128
CAP = 48
N_SEQ = 32
N_HEAD = 8
TOK = 1024
WIDE = 512
COLS = 256
SLOTS = N_SEQ * CAP
GROUPS = TOK // CH
PIECE = COLS // N_SEQ
EARLY = 16
MESH = pl.DeviceIdType.MESH
BF16 = jnp.bfloat16
F32 = jnp.float32

epsilon = 1e-05

K0, V0, K1, V1, Q0, Q1, R0, R1 = range(8)


def kernel(
    q_hbm, k_hbm, v_hbm, send_ref, receive_ref, resets_ref, out_ref,
    q_ref, k_ref, v_ref, columns,
    pack_send, place_send, pack_recv, place_recv,
    outbox, inbox, q_ctx, k_ctx, v_ctx, raw, kv, carried,
    state_out, state_in, prefix_out, prefix_in, keeps, scale_out, scale_in, scale_parts, slot_parts, partial, z_box,
    in_sem, bulk_ssem, bulk_rsem, st_ssem, st_rsem, pf_ssem, pf_rsem, row_ssem, row_rsem, z_ssem, z_rsem,
):
    me = lax.axis_index("seq")
    mine = lax.axis_index("head")

    barrier = pltpu.get_barrier_semaphore()

    @pl.loop(1, N_SEQ, unroll=True)
    def _(k):
        pl.semaphore_signal(
            barrier, inc=1, device_id={"seq": lax.rem(me + k, N_SEQ), "head": mine}, device_id_type=MESH
        )

    @pl.loop(1, N_HEAD, unroll=True)
    def _(k):
        pl.semaphore_signal(
            barrier, inc=1, device_id={"seq": me, "head": lax.rem(mine + k, N_HEAD)}, device_id_type=MESH
        )

    staged = [
        pltpu.make_async_copy(source, target, in_sem.at[i])
        for i, (source, target) in enumerate([(k_hbm, k_ref), (v_hbm, v_ref), (q_hbm, q_ref)])
    ]
    for copy in staged:
        copy.start()

    diagonal = (
        lax.broadcasted_iota(jnp.int32, (128, 128), 0) == lax.broadcasted_iota(jnp.int32, (128, 128), 1)
    )

    def to_column(row):
        return jnp.sum(jnp.where(diagonal, jnp.broadcast_to(row, (128, 128)), 0.0), axis=1, keepdims=True)

    def to_row(column):
        return jnp.sum(jnp.where(diagonal, jnp.broadcast_to(column, (128, 128)), 0.0), axis=0, keepdims=True)

    def build_pack(table_ref, pack):
        corner = diagonal[:CAP, :CAP]
        for d in range(N_SEQ):
            row = jnp.broadcast_to(table_ref[d : d + 1, :].astype(F32), (CAP, CAP))
            column = jnp.sum(jnp.where(corner, row, 0.0), axis=1, keepdims=True)
            spots = lax.broadcasted_iota(jnp.int32, (CAP, TOK), 1).astype(F32)
            pack[d * CAP : (d + 1) * CAP, :] = jnp.where(spots == column, 1.0, 0.0).astype(BF16)
            columns[d * CAP : (d + 1) * CAP, :] = column

    def build_place(place):
        for i in range(SLOTS // 128):
            row = to_row(columns[i * 128 : (i + 1) * 128, :])

            @pl.loop(0, TOK // 256)
            def _(j):
                spots = (lax.broadcasted_iota(jnp.int32, (256, 128), 0) + j * 256).astype(F32)
                place[pl.ds(pl.multiple_of(j * 256, 256), 256), i * 128 : (i + 1) * 128] = jnp.where(
                    spots == row, 1.0, 0.0
                ).astype(BF16)

    def pack_rows(pack, rows_ref, half, stage):
        @pl.loop(0, SLOTS // 384)
        def _(i):
            here = pl.ds(pl.multiple_of(i * 384, 384), 384)
            outbox[stage, here, :] = jnp.dot(
                pack[here, :], rows_ref[:, half * COLS : (half + 1) * COLS], preferred_element_type=F32
            ).astype(BF16)

    def place_rows(place, stage, rows_ref, half):
        @pl.loop(0, TOK // 256)
        def _(i):
            here = pl.ds(pl.multiple_of(i * 256, 256), 256)
            rows_ref[here, half * COLS : (half + 1) * COLS] = jnp.dot(
                place[here, :], inbox[stage], preferred_element_type=F32
            ).astype(BF16)

    def block(device):
        return pl.ds(pl.multiple_of(device * CAP, CAP), CAP)

    def send_bulk(stage, parts=(0, 1)):
        def send(part):
            def one(k):
                peer = lax.rem(me + 13 * k, N_SEQ)
                pltpu.make_async_remote_copy(
                    src_ref=outbox.at[stage, block(peer), :],
                    dst_ref=inbox.at[stage, block(me), :],
                    send_sem=bulk_ssem.at[stage, part],
                    recv_sem=bulk_rsem.at[stage],
                    device_id={"seq": peer, "head": mine},
                    device_id_type=MESH,
                ).start()

            return one

        if 0 in parts:
            pl.loop(1, EARLY + 1, unroll=True)(send(0))
            inbox[stage, block(me), :] = outbox[stage, block(me), :]
        if 1 in parts:
            pl.loop(EARLY + 1, N_SEQ, unroll=True)(send(1))

    def bulk_of(stage, blocks, part):
        rows = pl.ds(0, blocks * CAP)
        return pltpu.make_async_remote_copy(
            src_ref=outbox.at[stage, rows, :],
            dst_ref=inbox.at[stage, rows, :],
            send_sem=bulk_ssem.at[stage, part],
            recv_sem=bulk_rsem.at[stage],
            device_id={"seq": me, "head": mine},
            device_id_type=MESH,
        )

    def arrived(stage):
        bulk_of(stage, N_SEQ - 1, 0).wait_recv()

    def sent_early(stage):
        bulk_of(stage, EARLY, 0).wait_send()

    def sent_late(stage):
        bulk_of(stage, N_SEQ - 1 - EARLY, 1).wait_send()

    def send_small(source, target, half, ssem, rsem):
        @pl.loop(1, N_SEQ, unroll=True)
        def _(k):
            peer = lax.rem(me + 13 * k, N_SEQ)
            pltpu.make_async_remote_copy(
                src_ref=source.at[half, peer],
                dst_ref=target.at[half, me],
                send_sem=ssem.at[half],
                recv_sem=rsem.at[half],
                device_id={"seq": peer, "head": mine},
                device_id_type=MESH,
            ).start()

        target[half, me] = source[half, me]

    def all_small(source, target, half, ssem, rsem):
        return pltpu.make_async_remote_copy(
            src_ref=source.at[half, pl.ds(0, N_SEQ - 1)],
            dst_ref=target.at[half, pl.ds(0, N_SEQ - 1)],
            send_sem=ssem.at[half],
            recv_sem=rsem.at[half],
            device_id={"seq": me, "head": mine},
            device_id_type=MESH,
        )

    def send_rows(source_of, target, which):
        @pl.loop(1, N_SEQ, unroll=True)
        def _(k):
            peer = lax.rem(me + 13 * k, N_SEQ)
            pltpu.make_async_remote_copy(
                src_ref=source_of(peer),
                dst_ref=target.at[me],
                send_sem=row_ssem.at[which],
                recv_sem=row_rsem.at[which],
                device_id={"seq": peer, "head": mine},
                device_id_type=MESH,
            ).start()

    def all_rows(target, which):
        most = pl.ds(0, N_SEQ - 1)
        return pltpu.make_async_remote_copy(
            src_ref=target.at[most],
            dst_ref=target.at[most],
            send_sem=row_ssem.at[which],
            recv_sem=row_rsem.at[which],
            device_id={"seq": me, "head": mine},
            device_id_type=MESH,
        )

    def keep_of(group):
        return 1.0 - resets_ref[group].astype(F32)

    def group_states(half):
        state = [jnp.zeros((HD, HD), F32), jnp.zeros((HD, HD), F32)]
        for c in range(GROUPS):
            keep = keep_of(c)
            for h in range(2):
                cols = slice(half * COLS + h * HD, half * COLS + (h + 1) * HD)
                rows = slice(c * CH, (c + 1) * CH)
                group_kv = lax.dot_general(
                    k_ctx[rows, cols], v_ctx[rows, cols], (((0,), (0,)), ((), ())), preferred_element_type=F32
                )
                kv[half, c, h * HD : (h + 1) * HD, :] = group_kv
                state[h] = state[h] * keep + group_kv
        for h in range(2):
            state_out[half, h * 16 : (h + 1) * 16] = state[h].reshape(16, PIECE, HD)

    def prefixes(half):
        total = jnp.zeros((PIECE, HD), F32)
        for s in range(N_SEQ):
            prefix_out[half, s] = total
            total = state_in[half, s] + keeps[s] * total

    def attend(half):
        causal = (
            lax.broadcasted_iota(jnp.int32, (CH, CH), 0) >= lax.broadcasted_iota(jnp.int32, (CH, CH), 1)
        )
        for h in range(2):
            state = prefix_in[half, h * 16 : (h + 1) * 16].reshape(HD, HD)
            for c in range(GROUPS):
                state = state * keep_of(c)
                carried[half, c, h * HD : (h + 1) * HD, :] = state.astype(BF16)
                state = state + kv[half, c, h * HD : (h + 1) * HD, :]
        for c in range(GROUPS):
            rows = slice(c * CH, (c + 1) * CH)
            squares = jnp.zeros((CH, HD), F32)
            for h in range(2):
                cols = slice(half * COLS + h * HD, half * COLS + (h + 1) * HD)
                q = q_ctx[rows, cols]
                scores = lax.dot_general(
                    q, k_ctx[rows, cols], (((1,), (1,)), ((), ())), preferred_element_type=F32
                )
                weights = jnp.where(causal, scores, 0.0).astype(BF16)
                value = jnp.dot(q, carried[half, c, h * HD : (h + 1) * HD, :], preferred_element_type=F32)
                value = value + jnp.dot(weights, v_ctx[rows, cols], preferred_element_type=F32)
                squares = squares + value * value
                raw[rows, cols] = value.astype(BF16)
            row = to_row(jnp.sum(squares, axis=1, keepdims=True))
            if half == 0:
                partial[c : c + 1, :] = row
            else:
                z_box[mine, c : c + 1, :] = partial[c : c + 1, :] + row

    slots = (
        lax.broadcasted_iota(jnp.int32, (CAP, 128), 0) == lax.broadcasted_iota(jnp.int32, (CAP, 128), 1)
    )

    def three_terms(column, rows):
        lane = lax.broadcasted_iota(jnp.int32, (rows, 128), 1)
        rest = jnp.broadcast_to(column, (rows, 128))
        parts = jnp.zeros((rows, 128), F32)
        for i in range(3):
            term = rest.astype(BF16).astype(F32)
            parts = jnp.where(lane == i, term, parts)
            rest = rest - term
        return parts.astype(BF16)

    def split_scale(scale):
        for c in range(TOK // 128):
            scale_parts[c * 128 : (c + 1) * 128, :] = three_terms(to_column(scale[c : c + 1, :]), 128)

    def pack_scales():
        @pl.loop(0, SLOTS // 384)
        def _(i):
            here = pl.ds(pl.multiple_of(i * 384, 384), 384)
            parts = jnp.dot(pack_recv[here, :], scale_parts[...], preferred_element_type=F32)
            columns[here, :] = jnp.sum(parts, axis=1, keepdims=True)

        for d in range(N_SEQ):
            spread = jnp.broadcast_to(columns[d * CAP : (d + 1) * CAP, :], (CAP, 128))
            scale_out[d] = jnp.sum(jnp.where(slots, spread, 0.0), axis=0, keepdims=True)
        scale_in[me] = scale_out[me]

    def place_scales():
        for d in range(N_SEQ):
            spread = jnp.broadcast_to(scale_in[d], (CAP, 128))
            column = jnp.sum(jnp.where(slots, spread, 0.0), axis=1, keepdims=True)
            slot_parts[d * CAP : (d + 1) * CAP, :] = three_terms(column, CAP)

        @pl.loop(0, TOK // 256)
        def _(i):
            here = pl.ds(pl.multiple_of(i * 256, 256), 256)
            parts = jnp.dot(place_send[here, :], slot_parts[...], preferred_element_type=F32)
            columns[here, :] = jnp.sum(parts, axis=1, keepdims=True)

    def place_scaled(stage, half):
        @pl.loop(0, TOK // 256)
        def _(i):
            here = pl.ds(pl.multiple_of(i * 256, 256), 256)
            rows = jnp.dot(place_send[here, :], inbox[stage], preferred_element_type=F32)
            out_ref[here, half * COLS : (half + 1) * COLS] = (rows * columns[here, :]).astype(BF16)

    keep_all = jnp.float32(1.0)
    for c in range(GROUPS):
        keep_all = keep_all * keep_of(c)
    keeps[me] = jnp.broadcast_to(keep_all, (1, 128))
    build_pack(send_ref, pack_send)
    staged[0].wait()
    pack_rows(pack_send, k_ref, 0, K0)
    staged[1].wait()
    pack_rows(pack_send, v_ref, 0, V0)
    pl.semaphore_wait(barrier, N_SEQ - 1 + N_HEAD - 1)
    send_rows(lambda peer: keeps.at[me], keeps, 0)
    send_bulk(K0)
    send_bulk(V0)
    build_place(place_send)
    pack_rows(pack_send, k_ref, 1, K1)
    pack_rows(pack_send, v_ref, 1, V1)
    sent_late(K0)
    send_bulk(K1)
    staged[2].wait()
    pack_rows(pack_send, q_ref, 0, Q0)
    pack_rows(pack_send, q_ref, 1, Q1)
    build_pack(receive_ref, pack_recv)
    build_place(place_recv)
    arrived(K0)
    place_rows(place_recv, K0, k_ctx, 0)
    arrived(V0)
    place_rows(place_recv, V0, v_ctx, 0)
    group_states(0)
    send_small(state_out, state_in, 0, st_ssem, st_rsem)
    sent_early(K1)
    send_bulk(V1)
    arrived(K1)
    place_rows(place_recv, K1, k_ctx, 1)
    all_small(state_out, state_in, 0, st_ssem, st_rsem).wait_recv()
    all_rows(keeps, 0).wait_recv()
    prefixes(0)
    send_small(prefix_out, prefix_in, 0, pf_ssem, pf_rsem)
    sent_early(V1)
    send_bulk(Q0)
    arrived(V1)
    place_rows(place_recv, V1, v_ctx, 1)
    group_states(1)
    send_small(state_out, state_in, 1, st_ssem, st_rsem)
    sent_early(Q0)
    send_bulk(Q1)
    all_small(prefix_out, prefix_in, 0, pf_ssem, pf_rsem).wait_recv()
    arrived(Q0)
    place_rows(place_recv, Q0, q_ctx, 0)
    attend(0)
    all_small(state_out, state_in, 1, st_ssem, st_rsem).wait_recv()
    prefixes(1)
    send_small(prefix_out, prefix_in, 1, pf_ssem, pf_rsem)
    pack_rows(pack_recv, raw, 0, R0)
    send_bulk(R0, (0,))
    arrived(Q1)
    place_rows(place_recv, Q1, q_ctx, 1)
    all_small(prefix_out, prefix_in, 1, pf_ssem, pf_rsem).wait_recv()
    attend(1)

    @pl.loop(1, N_HEAD, unroll=True)
    def _(k):
        pltpu.make_async_remote_copy(
            src_ref=z_box.at[mine],
            dst_ref=z_box.at[mine],
            send_sem=z_ssem,
            recv_sem=z_rsem,
            device_id={"seq": me, "head": lax.rem(mine + k, N_HEAD)},
            device_id_type=MESH,
        ).start()

    all_z = pltpu.make_async_remote_copy(
        src_ref=z_box.at[pl.ds(0, N_HEAD - 1)],
        dst_ref=z_box.at[pl.ds(0, N_HEAD - 1)],
        send_sem=z_ssem,
        recv_sem=z_rsem,
        device_id={"seq": me, "head": mine},
        device_id_type=MESH,
    )
    send_bulk(R0, (1,))
    pack_rows(pack_recv, raw, 1, R1)
    send_bulk(R1, (0,))
    all_z.wait_recv()
    squares = z_box[0]
    for z in range(1, N_HEAD):
        squares = squares + z_box[z]
    split_scale(lax.rsqrt(squares / (H * HD) + epsilon))
    pack_scales()
    send_rows(lambda peer: scale_out.at[peer], scale_in, 1)
    send_bulk(R1, (1,))
    arrived(R0)
    all_rows(scale_in, 1).wait_recv()
    place_scales()
    place_scaled(R0, 0)
    arrived(R1)
    place_scaled(R1, 1)

    all_z.wait_send()
    for stage in (K0, V0, Q1, R0, R1):
        sent_early(stage)
    for stage in (V0, K1, V1, Q0, Q1, R0, R1):
        sent_late(stage)
    for half in range(2):
        all_small(state_out, state_in, half, st_ssem, st_rsem).wait_send()
        all_small(prefix_out, prefix_in, half, pf_ssem, pf_rsem).wait_send()
    all_rows(keeps, 0).wait_send()
    all_rows(scale_in, 1).wait_send()


def shards(query_vectors, key_vectors, value_vectors, send_slots, receive_slots, resets):
    vmem = pl.BlockSpec(memory_space=pltpu.VMEM)
    hbm = pl.BlockSpec(memory_space=pl.ANY)
    square = lambda rows, columns: pltpu.VMEM((rows, columns), BF16)
    row_of_each = lambda: pltpu.VMEM((N_SEQ, 1, 128), F32)
    return pl.pallas_call(
        kernel,
        name="attention",
        out_shape=pltpu.VMEM((TOK, WIDE), BF16),
        in_specs=[hbm, hbm, hbm, vmem, vmem, pl.BlockSpec(memory_space=pltpu.SMEM)],
        out_specs=vmem,
        scratch_shapes=[
            square(TOK, WIDE), square(TOK, WIDE), square(TOK, WIDE), pltpu.VMEM((SLOTS, 1), F32),
            square(SLOTS, TOK), square(TOK, SLOTS), square(SLOTS, TOK), square(TOK, SLOTS),
            pltpu.VMEM((8, SLOTS, COLS), BF16), pltpu.VMEM((8, SLOTS, COLS), BF16),
            square(TOK, WIDE), square(TOK, WIDE), square(TOK, WIDE), square(TOK, WIDE),
            pltpu.VMEM((2, GROUPS, COLS, HD), F32), pltpu.VMEM((2, GROUPS, COLS, HD), BF16),
            pltpu.VMEM((2, N_SEQ, PIECE, HD), F32), pltpu.VMEM((2, N_SEQ, PIECE, HD), F32),
            pltpu.VMEM((2, N_SEQ, PIECE, HD), F32), pltpu.VMEM((2, N_SEQ, PIECE, HD), F32),
            row_of_each(), row_of_each(), row_of_each(),
            square(TOK, 128), square(SLOTS, 128), pltpu.VMEM((TOK // 128, 128), F32), pltpu.VMEM((N_HEAD, TOK // 128, 128), F32),
            pltpu.SemaphoreType.DMA((3,)),
            pltpu.SemaphoreType.DMA((8, 2)), pltpu.SemaphoreType.DMA((8,)),
            pltpu.SemaphoreType.DMA((2,)), pltpu.SemaphoreType.DMA((2,)),
            pltpu.SemaphoreType.DMA((2,)), pltpu.SemaphoreType.DMA((2,)),
            pltpu.SemaphoreType.DMA((2,)), pltpu.SemaphoreType.DMA((2,)),
            pltpu.SemaphoreType.DMA, pltpu.SemaphoreType.DMA,
        ],
        compiler_params=pltpu.CompilerParams(
            collective_id=0, has_side_effects=True, vmem_limit_bytes=60 * 2**20
        ),
    )(query_vectors, key_vectors, value_vectors, send_slots, receive_slots, resets)


def solution(mesh):
    placed = (
        P("seq", "head"),
        P("seq", "head"),
        P("seq", "head"),
        P("seq", None),
        P("seq", None),
        P("seq"),
    )
    return jax.shard_map(shards, mesh=mesh, in_specs=placed, out_specs=P("seq", "head"), check_vma=False)
```

```python
import functools

import jax
import jax.numpy as jnp
from jax import lax
from jax.experimental import pallas as pl
from jax.experimental.pallas import tpu as pltpu
from jax.sharding import PartitionSpec as P

H = 32
HD = 128
CH = 128
CAP = 48
N_SEQ = 32
N_HEAD = 8
TOK = 1024
WIDE = 512
COLS = 256
SLOTS = N_SEQ * CAP
GROUPS = TOK // CH
PIECE = COLS // N_SEQ
EARLY = 16
MESH = pl.DeviceIdType.MESH
BF16 = jnp.bfloat16
F32 = jnp.float32

epsilon = 1e-05

K0, V0, K1, V1, Q0, Q1, R0, R1 = range(8)


def kernel(
    q_hbm, k_hbm, v_hbm, send_ref, receive_ref, resets_ref, out_ref,
    q_ref, k_ref, v_ref, columns,
    pack_send, place_send, pack_recv, place_recv,
    outbox, inbox, q_ctx, k_ctx, v_ctx, raw, kv, carried,
    state_out, state_in, prefix_out, prefix_in, keeps, scale_out, scale_in, scale_parts, slot_parts, partial, z_box,
    in_sem, bulk_ssem, bulk_rsem, st_ssem, st_rsem, pf_ssem, pf_rsem, row_ssem, row_rsem, z_ssem, z_rsem,
):
    me = lax.axis_index("seq")
    mine = lax.axis_index("head")

    barrier = pltpu.get_barrier_semaphore()

    @pl.loop(1, N_SEQ, unroll=True)
    def _(k):
        pl.semaphore_signal(
            barrier, inc=1, device_id={"seq": lax.rem(me + k, N_SEQ), "head": mine}, device_id_type=MESH
        )

    @pl.loop(1, N_HEAD, unroll=True)
    def _(k):
        pl.semaphore_signal(
            barrier, inc=1, device_id={"seq": me, "head": lax.rem(mine + k, N_HEAD)}, device_id_type=MESH
        )

    staged = [
        pltpu.make_async_copy(source, target, in_sem.at[i])
        for i, (source, target) in enumerate([(k_hbm, k_ref), (v_hbm, v_ref), (q_hbm, q_ref)])
    ]
    for copy in staged:
        copy.start()

    diagonal = (
        lax.broadcasted_iota(jnp.int32, (128, 128), 0) == lax.broadcasted_iota(jnp.int32, (128, 128), 1)
    )

    def to_column(row):
        return jnp.sum(jnp.where(diagonal, jnp.broadcast_to(row, (128, 128)), 0.0), axis=1, keepdims=True)

    def to_row(column):
        return jnp.sum(jnp.where(diagonal, jnp.broadcast_to(column, (128, 128)), 0.0), axis=0, keepdims=True)

    def build_pack(table_ref, pack):
        corner = diagonal[:CAP, :CAP]
        for d in range(N_SEQ):
            row = jnp.broadcast_to(table_ref[d : d + 1, :].astype(F32), (CAP, CAP))
            column = jnp.sum(jnp.where(corner, row, 0.0), axis=1, keepdims=True)
            spots = lax.broadcasted_iota(jnp.int32, (CAP, TOK), 1).astype(F32)
            pack[d * CAP : (d + 1) * CAP, :] = jnp.where(spots == column, 1.0, 0.0).astype(BF16)
            columns[d * CAP : (d + 1) * CAP, :] = column

    def build_place(place):
        for i in range(SLOTS // 128):
            row = to_row(columns[i * 128 : (i + 1) * 128, :])

            @pl.loop(0, TOK // 256)
            def _(j):
                spots = (lax.broadcasted_iota(jnp.int32, (256, 128), 0) + j * 256).astype(F32)
                place[pl.ds(pl.multiple_of(j * 256, 256), 256), i * 128 : (i + 1) * 128] = jnp.where(
                    spots == row, 1.0, 0.0
                ).astype(BF16)

    def pack_rows(pack, rows_ref, half, stage):
        @pl.loop(0, SLOTS // 384)
        def _(i):
            here = pl.ds(pl.multiple_of(i * 384, 384), 384)
            outbox[stage, here, :] = jnp.dot(
                pack[here, :], rows_ref[:, half * COLS : (half + 1) * COLS], preferred_element_type=F32
            ).astype(BF16)

    def place_rows(place, stage, rows_ref, half):
        @pl.loop(0, TOK // 256, unroll=True)
        def _(i):
            here = pl.ds(pl.multiple_of(i * 256, 256), 256)
            rows_ref[here, half * COLS : (half + 1) * COLS] = jnp.dot(
                place[here, :], inbox[stage], preferred_element_type=F32
            ).astype(BF16)

    def block(device):
        return pl.ds(pl.multiple_of(device * CAP, CAP), CAP)

    def send_bulk(stage, parts=(0, 1)):
        def send(part):
            def one(k):
                peer = lax.rem(me + 13 * k, N_SEQ)
                pltpu.make_async_remote_copy(
                    src_ref=outbox.at[stage, block(peer), :],
                    dst_ref=inbox.at[stage, block(me), :],
                    send_sem=bulk_ssem.at[stage, part],
                    recv_sem=bulk_rsem.at[stage],
                    device_id={"seq": peer, "head": mine},
                    device_id_type=MESH,
                ).start()

            return one

        if 0 in parts:
            pl.loop(1, EARLY + 1, unroll=True)(send(0))
            inbox[stage, block(me), :] = outbox[stage, block(me), :]
        if 1 in parts:
            pl.loop(EARLY + 1, N_SEQ, unroll=True)(send(1))

    def bulk_of(stage, blocks, part):
        rows = pl.ds(0, blocks * CAP)
        return pltpu.make_async_remote_copy(
            src_ref=outbox.at[stage, rows, :],
            dst_ref=inbox.at[stage, rows, :],
            send_sem=bulk_ssem.at[stage, part],
            recv_sem=bulk_rsem.at[stage],
            device_id={"seq": me, "head": mine},
            device_id_type=MESH,
        )

    def arrived(stage):
        bulk_of(stage, N_SEQ - 1, 0).wait_recv()

    def sent_early(stage):
        bulk_of(stage, EARLY, 0).wait_send()

    def sent_late(stage):
        bulk_of(stage, N_SEQ - 1 - EARLY, 1).wait_send()

    def send_small(source, target, half, ssem, rsem):
        @pl.loop(1, N_SEQ, unroll=True)
        def _(k):
            peer = lax.rem(me + 13 * k, N_SEQ)
            pltpu.make_async_remote_copy(
                src_ref=source.at[half, peer],
                dst_ref=target.at[half, me],
                send_sem=ssem.at[half],
                recv_sem=rsem.at[half],
                device_id={"seq": peer, "head": mine},
                device_id_type=MESH,
            ).start()

        target[half, me] = source[half, me]

    def all_small(source, target, half, ssem, rsem):
        return pltpu.make_async_remote_copy(
            src_ref=source.at[half, pl.ds(0, N_SEQ - 1)],
            dst_ref=target.at[half, pl.ds(0, N_SEQ - 1)],
            send_sem=ssem.at[half],
            recv_sem=rsem.at[half],
            device_id={"seq": me, "head": mine},
            device_id_type=MESH,
        )

    def send_rows(source_of, target, which):
        @pl.loop(1, N_SEQ, unroll=True)
        def _(k):
            peer = lax.rem(me + 13 * k, N_SEQ)
            pltpu.make_async_remote_copy(
                src_ref=source_of(peer),
                dst_ref=target.at[me],
                send_sem=row_ssem.at[which],
                recv_sem=row_rsem.at[which],
                device_id={"seq": peer, "head": mine},
                device_id_type=MESH,
            ).start()

    def all_rows(target, which):
        most = pl.ds(0, N_SEQ - 1)
        return pltpu.make_async_remote_copy(
            src_ref=target.at[most],
            dst_ref=target.at[most],
            send_sem=row_ssem.at[which],
            recv_sem=row_rsem.at[which],
            device_id={"seq": me, "head": mine},
            device_id_type=MESH,
        )

    def keep_of(group):
        return 1.0 - resets_ref[group].astype(F32)

    def group_states(half):
        state = [jnp.zeros((HD, HD), F32), jnp.zeros((HD, HD), F32)]
        for c in range(GROUPS):
            keep = keep_of(c)
            for h in range(2):
                cols = slice(half * COLS + h * HD, half * COLS + (h + 1) * HD)
                rows = slice(c * CH, (c + 1) * CH)
                group_kv = lax.dot_general(
                    k_ctx[rows, cols], v_ctx[rows, cols], (((0,), (0,)), ((), ())), preferred_element_type=F32
                )
                kv[half, c, h * HD : (h + 1) * HD, :] = group_kv
                state[h] = state[h] * keep + group_kv
        for h in range(2):
            state_out[half, h * 16 : (h + 1) * 16] = state[h].reshape(16, PIECE, HD)

    def prefixes(half):
        total = jnp.zeros((PIECE, HD), F32)
        for s in range(N_SEQ):
            prefix_out[half, s] = total
            total = state_in[half, s] + keeps[s] * total

    def attend(half):
        causal = (
            lax.broadcasted_iota(jnp.int32, (CH, CH), 0) >= lax.broadcasted_iota(jnp.int32, (CH, CH), 1)
        )
        for h in range(2):
            state = prefix_in[half, h * 16 : (h + 1) * 16].reshape(HD, HD)
            for c in range(GROUPS):
                state = state * keep_of(c)
                carried[half, c, h * HD : (h + 1) * HD, :] = state.astype(BF16)
                state = state + kv[half, c, h * HD : (h + 1) * HD, :]
        for c in range(GROUPS):
            rows = slice(c * CH, (c + 1) * CH)
            squares = jnp.zeros((CH, HD), F32)
            for h in range(2):
                cols = slice(half * COLS + h * HD, half * COLS + (h + 1) * HD)
                q = q_ctx[rows, cols]
                scores = lax.dot_general(
                    q, k_ctx[rows, cols], (((1,), (1,)), ((), ())), preferred_element_type=F32
                )
                weights = jnp.where(causal, scores, 0.0).astype(BF16)
                value = jnp.dot(q, carried[half, c, h * HD : (h + 1) * HD, :], preferred_element_type=F32)
                value = value + jnp.dot(weights, v_ctx[rows, cols], preferred_element_type=F32)
                squares = squares + value * value
                raw[rows, cols] = value.astype(BF16)
            row = to_row(jnp.sum(squares, axis=1, keepdims=True))
            if half == 0:
                partial[c : c + 1, :] = row
            else:
                z_box[mine, c : c + 1, :] = partial[c : c + 1, :] + row

    slots = (
        lax.broadcasted_iota(jnp.int32, (CAP, 128), 0) == lax.broadcasted_iota(jnp.int32, (CAP, 128), 1)
    )

    def three_terms(column, rows):
        lane = lax.broadcasted_iota(jnp.int32, (rows, 128), 1)
        rest = jnp.broadcast_to(column, (rows, 128))
        parts = jnp.zeros((rows, 128), F32)
        for i in range(3):
            term = rest.astype(BF16).astype(F32)
            parts = jnp.where(lane == i, term, parts)
            rest = rest - term
        return parts.astype(BF16)

    def split_scale(scale):
        for c in range(TOK // 128):
            scale_parts[c * 128 : (c + 1) * 128, :] = three_terms(to_column(scale[c : c + 1, :]), 128)

    def pack_scales():
        @pl.loop(0, SLOTS // 384)
        def _(i):
            here = pl.ds(pl.multiple_of(i * 384, 384), 384)
            parts = jnp.dot(pack_recv[here, :], scale_parts[...], preferred_element_type=F32)
            columns[here, :] = jnp.sum(parts, axis=1, keepdims=True)

        for d in range(N_SEQ):
            spread = jnp.broadcast_to(columns[d * CAP : (d + 1) * CAP, :], (CAP, 128))
            scale_out[d] = jnp.sum(jnp.where(slots, spread, 0.0), axis=0, keepdims=True)
        scale_in[me] = scale_out[me]

    def place_scales():
        for d in range(N_SEQ):
            spread = jnp.broadcast_to(scale_in[d], (CAP, 128))
            column = jnp.sum(jnp.where(slots, spread, 0.0), axis=1, keepdims=True)
            slot_parts[d * CAP : (d + 1) * CAP, :] = three_terms(column, CAP)

        @pl.loop(0, TOK // 256)
        def _(i):
            here = pl.ds(pl.multiple_of(i * 256, 256), 256)
            parts = jnp.dot(place_send[here, :], slot_parts[...], preferred_element_type=F32)
            columns[here, :] = jnp.sum(parts, axis=1, keepdims=True)

    def place_scaled(stage, half):
        @pl.loop(0, TOK // 256, unroll=True)
        def _(i):
            here = pl.ds(pl.multiple_of(i * 256, 256), 256)
            rows = jnp.dot(place_send[here, :], inbox[stage], preferred_element_type=F32)
            out_ref[here, half * COLS : (half + 1) * COLS] = (rows * columns[here, :]).astype(BF16)

    keep_all = jnp.float32(1.0)
    for c in range(GROUPS):
        keep_all = keep_all * keep_of(c)
    keeps[me] = jnp.broadcast_to(keep_all, (1, 128))
    build_pack(send_ref, pack_send)
    staged[0].wait()
    pack_rows(pack_send, k_ref, 0, K0)
    staged[1].wait()
    pack_rows(pack_send, v_ref, 0, V0)
    pl.semaphore_wait(barrier, N_SEQ - 1 + N_HEAD - 1)
    send_rows(lambda peer: keeps.at[me], keeps, 0)
    send_bulk(K0)
    send_bulk(V0)
    build_place(place_send)
    pack_rows(pack_send, k_ref, 1, K1)
    pack_rows(pack_send, v_ref, 1, V1)
    sent_late(K0)
    send_bulk(K1)
    staged[2].wait()
    pack_rows(pack_send, q_ref, 0, Q0)
    pack_rows(pack_send, q_ref, 1, Q1)
    build_pack(receive_ref, pack_recv)
    build_place(place_recv)
    arrived(K0)
    place_rows(place_recv, K0, k_ctx, 0)
    arrived(V0)
    place_rows(place_recv, V0, v_ctx, 0)
    group_states(0)
    send_small(state_out, state_in, 0, st_ssem, st_rsem)
    sent_early(K1)
    send_bulk(V1)
    arrived(K1)
    place_rows(place_recv, K1, k_ctx, 1)
    all_small(state_out, state_in, 0, st_ssem, st_rsem).wait_recv()
    all_rows(keeps, 0).wait_recv()
    prefixes(0)
    send_small(prefix_out, prefix_in, 0, pf_ssem, pf_rsem)
    sent_early(V1)
    send_bulk(Q0)
    arrived(V1)
    place_rows(place_recv, V1, v_ctx, 1)
    group_states(1)
    send_small(state_out, state_in, 1, st_ssem, st_rsem)
    sent_early(Q0)
    send_bulk(Q1)
    all_small(prefix_out, prefix_in, 0, pf_ssem, pf_rsem).wait_recv()
    arrived(Q0)
    place_rows(place_recv, Q0, q_ctx, 0)
    attend(0)
    all_small(state_out, state_in, 1, st_ssem, st_rsem).wait_recv()
    prefixes(1)
    send_small(prefix_out, prefix_in, 1, pf_ssem, pf_rsem)
    pack_rows(pack_recv, raw, 0, R0)
    send_bulk(R0, (0,))
    arrived(Q1)
    place_rows(place_recv, Q1, q_ctx, 1)
    all_small(prefix_out, prefix_in, 1, pf_ssem, pf_rsem).wait_recv()
    attend(1)

    @pl.loop(1, N_HEAD, unroll=True)
    def _(k):
        pltpu.make_async_remote_copy(
            src_ref=z_box.at[mine],
            dst_ref=z_box.at[mine],
            send_sem=z_ssem,
            recv_sem=z_rsem,
            device_id={"seq": me, "head": lax.rem(mine + k, N_HEAD)},
            device_id_type=MESH,
        ).start()

    all_z = pltpu.make_async_remote_copy(
        src_ref=z_box.at[pl.ds(0, N_HEAD - 1)],
        dst_ref=z_box.at[pl.ds(0, N_HEAD - 1)],
        send_sem=z_ssem,
        recv_sem=z_rsem,
        device_id={"seq": me, "head": mine},
        device_id_type=MESH,
    )
    send_bulk(R0, (1,))
    pack_rows(pack_recv, raw, 1, R1)
    send_bulk(R1, (0,))
    all_z.wait_recv()
    squares = z_box[0]
    for z in range(1, N_HEAD):
        squares = squares + z_box[z]
    split_scale(lax.rsqrt(squares / (H * HD) + epsilon))
    pack_scales()
    send_rows(lambda peer: scale_out.at[peer], scale_in, 1)
    send_bulk(R1, (1,))
    arrived(R0)
    all_rows(scale_in, 1).wait_recv()
    place_scales()
    place_scaled(R0, 0)
    arrived(R1)
    place_scaled(R1, 1)

    all_z.wait_send()
    for stage in (K0, V0, Q1, R0, R1):
        sent_early(stage)
    for stage in (V0, K1, V1, Q0, Q1, R0, R1):
        sent_late(stage)
    for half in range(2):
        all_small(state_out, state_in, half, st_ssem, st_rsem).wait_send()
        all_small(prefix_out, prefix_in, half, pf_ssem, pf_rsem).wait_send()
    all_rows(keeps, 0).wait_send()
    all_rows(scale_in, 1).wait_send()


def shards(query_vectors, key_vectors, value_vectors, send_slots, receive_slots, resets):
    vmem = pl.BlockSpec(memory_space=pltpu.VMEM)
    hbm = pl.BlockSpec(memory_space=pl.ANY)
    square = lambda rows, columns: pltpu.VMEM((rows, columns), BF16)
    row_of_each = lambda: pltpu.VMEM((N_SEQ, 1, 128), F32)
    return pl.pallas_call(
        kernel,
        name="attention",
        out_shape=pltpu.VMEM((TOK, WIDE), BF16),
        in_specs=[hbm, hbm, hbm, vmem, vmem, pl.BlockSpec(memory_space=pltpu.SMEM)],
        out_specs=vmem,
        scratch_shapes=[
            square(TOK, WIDE), square(TOK, WIDE), square(TOK, WIDE), pltpu.VMEM((SLOTS, 1), F32),
            square(SLOTS, TOK), square(TOK, SLOTS), square(SLOTS, TOK), square(TOK, SLOTS),
            pltpu.VMEM((8, SLOTS, COLS), BF16), pltpu.VMEM((8, SLOTS, COLS), BF16),
            square(TOK, WIDE), square(TOK, WIDE), square(TOK, WIDE), square(TOK, WIDE),
            pltpu.VMEM((2, GROUPS, COLS, HD), F32), pltpu.VMEM((2, GROUPS, COLS, HD), BF16),
            pltpu.VMEM((2, N_SEQ, PIECE, HD), F32), pltpu.VMEM((2, N_SEQ, PIECE, HD), F32),
            pltpu.VMEM((2, N_SEQ, PIECE, HD), F32), pltpu.VMEM((2, N_SEQ, PIECE, HD), F32),
            row_of_each(), row_of_each(), row_of_each(),
            square(TOK, 128), square(SLOTS, 128), pltpu.VMEM((TOK // 128, 128), F32), pltpu.VMEM((N_HEAD, TOK // 128, 128), F32),
            pltpu.SemaphoreType.DMA((3,)),
            pltpu.SemaphoreType.DMA((8, 2)), pltpu.SemaphoreType.DMA((8,)),
            pltpu.SemaphoreType.DMA((2,)), pltpu.SemaphoreType.DMA((2,)),
            pltpu.SemaphoreType.DMA((2,)), pltpu.SemaphoreType.DMA((2,)),
            pltpu.SemaphoreType.DMA((2,)), pltpu.SemaphoreType.DMA((2,)),
            pltpu.SemaphoreType.DMA, pltpu.SemaphoreType.DMA,
        ],
        compiler_params=pltpu.CompilerParams(
            collective_id=0, has_side_effects=True, vmem_limit_bytes=60 * 2**20
        ),
    )(query_vectors, key_vectors, value_vectors, send_slots, receive_slots, resets)


def solution(mesh):
    placed = (
        P("seq", "head"),
        P("seq", "head"),
        P("seq", "head"),
        P("seq", None),
        P("seq", None),
        P("seq"),
    )
    return jax.shard_map(shards, mesh=mesh, in_specs=placed, out_specs=P("seq", "head"), check_vma=False)
```
